32 devices in a mesh: section: 4 (over z), dp: 2 (over x), tensor: 4 (over y, core).
Axes of the slice: x: 2, y: 2, z: 4, core: 2. Of those that a mesh axis runs over, the one named last changes fastest.
Arguments:
- inputs: float32 [4, 2, 256, 768], P('section', 'dp'), may hold values from -6 to 6
- segments: int32 [4, 2, 256], P(None, 'dp'), may hold values from -1 to 6, as said below
- cotangent: float32 [4, 2, 256, 768], P('section', 'dp'), may hold values from -6 to 6
- norm_gain: float32 [4, 768], P('section'), may hold values from 0.1 to 1.9
- norm_shift: float32 [4, 768], P('section'), may hold values from -3 to 3
- out_bias: float32 [4, 768], P('section'), may hold values from -3 to 3
- attn_qkv: float32 [2, 768, 3, 768], P(None, 'dp', None, 'tensor'), may hold values from -0.21875 to 0.21875
- attn_out: float32 [2, 768, 768], P(None, 'dp', 'tensor'), may hold values from -1.25 to 1.25
- attn_bias: float32 [2, 2, 768], P(None, None, 'tensor'), may hold values from -3 to 3
- mlp_in: float32 [2, 768, 3072], P(None, 'dp', 'tensor'), may hold values from -0.21875 to 0.21875
- mlp_out: float32 [2, 3072, 768], P(None, 'tensor', 'dp'), may hold values from -0.109375 to 0.109375
- mlp_bias: float32 [2, 3072], P(None, 'tensor'), may hold values from -3 to 3
Outputs:
- outputs: float32 [4, 2, 256, 768], P('section', 'dp')
- input_grad: float32 [4, 2, 256, 768], P('section', 'dp')
- norm_gain_grad: float32 [4, 768], P('section')
- norm_shift_grad: float32 [4, 768], P('section')
- out_bias_grad: float32 [4, 768], P('section')
- attn_qkv_grad: float32 [2, 768, 3, 768], P(None, 'dp', None, 'tensor')
- attn_out_grad: float32 [2, 768, 768], P(None, 'dp', 'tensor')
- attn_bias_grad: float32 [2, 2, 768], P(None, None, 'tensor')
- mlp_in_grad: float32 [2, 768, 3072], P(None, 'dp', 'tensor')
- mlp_out_grad: float32 [2, 3072, 768], P(None, 'tensor', 'dp')
- mlp_bias_grad: float32 [2, 3072], P(None, 'tensor')
The draws below stay inside these ranges and needn't reach their ends.
Inputs may be any that keep to these rules, and one draw needn't show every extreme that they name: `segments`: each row holds 7 images numbered 0 to 6 in order, each of 36 consecutive slots; the remaining 4 slots are -1 and lie before, between or after images.
All inputs are finite; a program needn't handle non-finite values.
Results may differ from the reference program's by a relative error of at most 0.02.
Values may be sent and summed in bfloat16 or wider, within the bound.
No kernel may reach another device: no remote copies, remote signals or barrier semaphores. Data moves between devices by JAX's collectives and lax.ppermute only.
A program may use at most 192 MiB of HBM per device.

```python
import jax
import jax.numpy as jnp
from jax import lax

D = 768
HEADS = 12
HEAD = 64
FF = 3072
LAYERS = 2
PATCHES = 36
IMAGES = 7
PADDING = 4
SLOTS = 256
MICRO = 4
ROWS = 2
N_SECTION = 4


def draw_segments(key, part):
    key = jax.random.fold_in(key, 11)
    gap_choice = jax.random.randint(key, (MICRO, ROWS, PADDING), 0, IMAGES + 1)
    gap_counts = jnp.sum((gap_choice[..., None] == jnp.arange(IMAGES + 1)).astype(jnp.int32), axis=-2)
    before = jnp.cumsum(gap_counts, axis=-1)[..., :IMAGES]
    starts = before + PATCHES * jnp.arange(IMAGES)
    places = jnp.arange(SLOTS)
    inside = (places >= starts[..., None]) & (places < starts[..., None] + PATCHES)
    numbers = jnp.arange(IMAGES)[:, None] + 1
    ident = jnp.sum(jnp.where(inside, numbers, 0), axis=-2) - 1
    return ident.astype(jnp.int32)


def block_scale(key, shape, shards, low, largest):
    factor_of = 1.0
    for position, blocks in shards:
        steps = jax.random.uniform(jax.random.fold_in(jax.random.fold_in(key, 6), position), (blocks,), jnp.float32, low / len(shards), largest / len(shards))
        factor_of = factor_of * jnp.repeat(jnp.exp(steps), shape[position] // blocks).reshape((-1,) + (1,) * (len(shape) - 1 - position))
    return factor_of


def bell_draw(stream_key, dims, width, bound, split=(), dtype=jnp.bfloat16):
    loudness = block_scale(stream_key, dims, split, -0.22, 0.18) if split else 1.0
    entries = jax.random.normal(stream_key, dims, jnp.float32) * width * loudness
    return jnp.minimum(jnp.maximum(entries, -bound), bound).astype(dtype)


def setup_inputs(seed: int = 0) -> dict:
    arg_keys = jax.random.split(jax.random.key(seed), 13)
    inputs = bell_draw(arg_keys[0], (MICRO, ROWS, SLOTS, D), 1.0, 6.0, ((0, 4), (1, 2)), jnp.float32)
    segments = draw_segments(jax.random.fold_in(arg_keys[12], 71), 0)
    cotangent = bell_draw(arg_keys[2], (MICRO, ROWS, SLOTS, D), 1.0, 6.0, ((0, 4), (1, 2)), jnp.float32)
    norm_gain = jnp.clip(1.0 + 0.18 * jax.random.normal(arg_keys[3], (2 * LAYERS, D), jnp.float32), 0.1, 1.9)
    norm_shift = bell_draw(arg_keys[4], (2 * LAYERS, D), 0.5, 3.0, ((0, 4),), jnp.float32)
    out_bias = bell_draw(arg_keys[5], (2 * LAYERS, D), 0.5, 3.0, ((0, 4),), jnp.float32)
    attn_qkv = bell_draw(arg_keys[6], (LAYERS, D, 3, D), D ** -0.5, 0.21875, ((1, 2), (3, 4)), jnp.float32)
    attn_out = bell_draw(arg_keys[7], (LAYERS, D, D), (D // PATCHES) ** -0.5, 1.25, ((1, 2), (2, 4)), jnp.float32)
    attn_bias = bell_draw(arg_keys[8], (LAYERS, 2, D), 0.5, 3.0, ((2, 4),), jnp.float32)
    mlp_in = bell_draw(arg_keys[9], (LAYERS, D, FF), D ** -0.5, 0.21875, ((1, 2), (2, 4)), jnp.float32)
    mlp_out = bell_draw(arg_keys[10], (LAYERS, FF, D), FF ** -0.5, 0.109375, ((1, 4), (2, 2)), jnp.float32)
    mlp_bias = bell_draw(arg_keys[11], (LAYERS, FF), 0.5, 3.0, ((1, 4),), jnp.float32)
    return {"inputs": inputs, "segments": segments, "cotangent": cotangent, "norm_gain": norm_gain, "norm_shift": norm_shift, "out_bias": out_bias, "attn_qkv": attn_qkv, "attn_out": attn_out, "attn_bias": attn_bias, "mlp_in": mlp_in, "mlp_out": mlp_out, "mlp_bias": mlp_bias}


eps = 1e-06
masked_score = -1e+30
highest = lax.Precision.HIGHEST

@jax.custom_vjp
def low(v):
    return lax.optimization_barrier(v.astype(jnp.bfloat16)).astype(jnp.float32)

@jax.custom_vjp
def low_back(v):
    return v

def low_keep(v):
    return (low(v), None)

def low_pass(kept, grad):
    return (grad,)

def back_keep(v):
    return (v, None)

def back_low(kept, grad):
    return (low(grad),)
low.defvjp(low_keep, low_pass)
low_back.defvjp(back_keep, back_low)

def layer_norm(row_block, gain_row, shift_row):
    center = row_block - lax.optimization_barrier(jnp.mean(row_block, axis=-1, keepdims=True))
    spread = lax.optimization_barrier(jnp.mean(center * center, axis=-1, keepdims=True))
    return center * lax.rsqrt(spread + eps) * gain_row + shift_row

def attention(lowered, same_image, qkv_master, out_master, inner_bias):
    row_count, slot_count, model_width = lowered.shape
    w_query = low(qkv_master[:, 0, :])
    w_key = low(qkv_master[:, 1, :])
    w_value = low(qkv_master[:, 2, :])
    queries = low_back(low(jnp.einsum('rsd,de->rse', lowered, w_query, precision=highest) + inner_bias[0]))
    keys_all = low_back(low(jnp.einsum('rsd,de->rse', lowered, w_key, precision=highest)))
    values = low_back(low(jnp.einsum('rsd,de->rse', lowered, w_value, precision=highest) + inner_bias[1]))
    query_heads = queries.reshape(row_count, slot_count, HEADS, HEAD)
    key_heads = keys_all.reshape(row_count, slot_count, HEADS, HEAD)
    value_heads = values.reshape(row_count, slot_count, HEADS, HEAD)
    raw_scores = jnp.einsum('rqhd,rkhd->rhqk', query_heads, key_heads, precision=highest) * HEAD ** (-0.5)
    scores = jnp.where(same_image[:, None], low_back(raw_scores), masked_score)
    top_score = lax.optimization_barrier(jnp.max(scores, axis=-1, keepdims=True))
    expanded = jnp.exp(scores - top_score)
    soft_low = low(expanded / lax.optimization_barrier(jnp.sum(expanded, axis=-1, keepdims=True)))
    context = jnp.einsum('rhqk,rkhd->rqhd', soft_low, value_heads, precision=highest)
    context = low_back(low(context.reshape(row_count, slot_count, model_width)))
    return jnp.einsum('rse,de->rsd', context, low(out_master), precision=highest)

def feed_forward(lowered, up_master, down_master, up_bias):
    hidden = low_back(jnp.einsum('rsd,df->rsf', lowered, low(up_master), precision=highest) + up_bias)
    active = low(jax.nn.gelu(hidden, approximate=False))
    return jnp.einsum('rsf,fd->rsd', active, low(down_master), precision=highest)

def sub_layers(row_block, same_image, weights_all):
    gains, shifts, out_biases, qkv_masters, out_masters, attn_biases, up_masters, down_masters, up_biases = weights_all
    for section_number in range(N_SECTION):
        layer_number = section_number // 2
        lowered = low(layer_norm(row_block, gains[section_number], shifts[section_number]))
        if section_number % 2 == 0:
            branch = attention(lowered, same_image, qkv_masters[layer_number], out_masters[layer_number], attn_biases[layer_number])
        else:
            branch = feed_forward(lowered, up_masters[layer_number], down_masters[layer_number], up_biases[layer_number])
        row_block = row_block + (low_back(branch) + out_biases[section_number])
    return row_block

def reference(inputs, segments, cotangent, norm_gain, norm_shift, out_bias, attn_qkv, attn_out, attn_bias, mlp_in, mlp_out, mlp_bias):
    same_all = segments[:, :, :, None] == segments[:, :, None, :]
    params = (norm_gain, norm_shift, out_bias, attn_qkv, attn_out, attn_bias, mlp_in, mlp_out, mlp_bias)

    def whole(row_all, weights_all):
        step_fn = jax.checkpoint(sub_layers)

        def one_micro(carried, pair_items):
            return (carried, step_fn(pair_items[0], pair_items[1], weights_all))
        unused, result = lax.scan(one_micro, jnp.zeros((), jnp.float32), (row_all, same_all))
        return result
    outputs, pullback = jax.vjp(whole, inputs, params)
    input_grad, grads = pullback(cotangent)
    return (outputs, input_grad, grads[0], grads[1], grads[2], grads[3], grads[4], grads[5], grads[6], grads[7], grads[8])
```

```python
import functools

import jax
import jax.numpy as jnp
from jax import lax
from jax.experimental import pallas as pl
from jax.experimental.pallas import tpu as pltpu
from jax.sharding import PartitionSpec as P

HEAD = 64
EPS = 1e-06
MASKED = -1e30
BF16 = jnp.bfloat16
F32 = jnp.float32
VMEM_LIMIT = 40 * 1024 * 1024


def dot_ab(a, b):
    return lax.dot_general(a, b, (((1,), (0,)), ((), ())), preferred_element_type=F32)


def dot_abt(a, b):
    return lax.dot_general(a, b, (((1,), (1,)), ((), ())), preferred_element_type=F32)


def dot_atb(a, b):
    return lax.dot_general(a, b, (((0,), (0,)), ((), ())), preferred_element_type=F32)


def normalized(x):
    center = x - jnp.mean(x, axis=-1, keepdims=True)
    rstd = lax.rsqrt(jnp.mean(center * center, axis=-1, keepdims=True) + EPS)
    return center * rstd, rstd


def put_halves(scal, dst, mine, other):
    half = mine.shape[0]
    core = scal[0]
    dst[pl.ds(pl.multiple_of(core * half, half), half), :] = mine[...].astype(F32)
    dst[pl.ds(pl.multiple_of((1 - core) * half, half), half), :] = other[...].astype(F32)


def take_halves(scal, src, mine, other):
    half = mine.shape[0]
    core = scal[0]
    mine[...] = src[pl.ds(pl.multiple_of(core * half, half), half), :].astype(BF16)
    other[...] = src[pl.ds(pl.multiple_of((1 - core) * half, half), half), :].astype(BF16)


def fill_rows(scal, dst, pieces):
    if len(pieces) == 1:
        dst[...] = pieces[0][...]
        return
    own, near, far = pieces
    half, part = own.shape[0], near.shape[0]
    dp, parity = scal[1], scal[2]
    dst[pl.ds(pl.multiple_of(dp * half, part), half), :] = own[...]
    peer = (1 - dp) * half
    dst[pl.ds(pl.multiple_of(peer + parity * part, part), part), :] = near[...]
    dst[pl.ds(pl.multiple_of(peer + (1 - parity) * part, part), part), :] = far[...]


def fill_columns(scal, dst, pieces):
    if len(pieces) == 1:
        dst[...] = pieces[0][...]
        return
    own, near, far = pieces
    half, part = own.shape[1], near.shape[0]
    dp, parity = scal[1], scal[2]
    dst[:, pl.ds(pl.multiple_of(dp * half, 128), half)] = own[...]
    peer = pl.multiple_of((1 - dp) * half, 128)
    dst[pl.ds(pl.multiple_of(parity * part, part), part), pl.ds(peer, half)] = near[...]
    dst[pl.ds(pl.multiple_of((1 - parity) * part, part), part), pl.ds(peer, half)] = far[...]


def residual(scal, first, refs, x_out):
    if first:
        x_out[...] = refs[0][...]
    else:
        x_prev, mine, other, bias = refs
        put_halves(scal, x_out, mine, other)
        x_out[...] = x_prev[...] + (x_out[...] + bias[...])
    return x_out[...]


def head_mask(width):
    return lax.broadcasted_iota(jnp.int32, (1, width), 1) // HEAD


def only(mask, values):
    return jnp.where(mask, values, jnp.zeros((), values.dtype))


def attn_forward(first, pieces, scal, *refs):
    res_count = 1 if first else 4
    res, refs = refs[:res_count], refs[res_count:]
    (gain, shift, seg_col, seg_row, inner), refs = refs[:5], refs[5:]
    weights, refs = refs[:pieces], refs[pieces:]
    x_out, low_out, w_out, q_out, k_out, v_out, soft_out, ctx_out, mine, other, total = refs
    x = residual(scal, first, res, x_out)
    fill_rows(scal, w_out, weights)
    xhat, _ = normalized(x)
    low = (xhat * gain[...] + shift[...]).astype(BF16)
    low_out[...] = low
    width = q_out.shape[1]
    qkv = dot_ab(low, w_out[:, : 3 * width])
    q = (qkv[:, :width] + inner[0:1, :]).astype(BF16)
    k = qkv[:, width : 2 * width].astype(BF16)
    v = (qkv[:, 2 * width :] + inner[1:2, :]).astype(BF16)
    q_out[...] = q
    k_out[...] = k
    v_out[...] = v
    same = seg_col[...] == seg_row[...]
    heads = head_mask(width)
    context = jnp.zeros((x.shape[0], width), F32)
    for h in range(width // HEAD):
        scores = dot_abt(only(heads == h, q), k) * HEAD ** (-0.5)
        scores = jnp.where(same, scores, MASKED)
        expanded = jnp.exp(scores - jnp.max(scores, axis=-1, keepdims=True))
        soft = expanded / jnp.sum(expanded, axis=-1, keepdims=True)
        soft_out[h] = soft
        context = context + dot_ab(soft.astype(BF16), only(heads == h, v))
    context = context.astype(BF16)
    ctx_out[...] = context
    total[...] = dot_abt(context, w_out[:, 3 * width :])
    take_halves(scal, total, mine, other)


def mlp_forward(pieces, scal, *refs):
    res, refs = refs[:4], refs[4:]
    (gain, shift, up_bias), refs = refs[:3], refs[3:]
    up_pieces, refs = refs[:pieces], refs[pieces:]
    down_pieces, refs = refs[:pieces], refs[pieces:]
    x_out, low_out, up_out, down_out, active_out, slope_out, mine, other, total = refs
    x = residual(scal, False, res, x_out)
    fill_rows(scal, up_out, up_pieces)
    fill_columns(scal, down_out, down_pieces)
    xhat, _ = normalized(x)
    low = (xhat * gain[...] + shift[...]).astype(BF16)
    low_out[...] = low
    hidden = dot_ab(low, up_out[...]) + up_bias[...]
    phi = 0.5 * (1.0 + lax.erf(hidden * 0.7071067811865476))
    slope_out[...] = phi + hidden * (0.3989422804014327 * jnp.exp(-0.5 * hidden * hidden))
    active = (hidden * phi).astype(BF16)
    active_out[...] = active
    total[...] = dot_ab(active, down_out[...])
    take_halves(scal, total, mine, other)


def norm_backward(scal, refs, g_out, small):
    g_prev, mine, other, x_next, gain = refs
    put_halves(scal, g_out, mine, other)
    d_normed = g_out[...]
    xhat, rstd = normalized(x_next[...])
    small[0:1, :] = jnp.sum(d_normed * xhat, axis=0, keepdims=True)
    small[1:2, :] = jnp.sum(d_normed, axis=0, keepdims=True)
    d_hat = d_normed * gain[...]
    inner = jnp.mean(d_hat * xhat, axis=-1, keepdims=True)
    g = g_prev[...] + (d_hat - jnp.mean(d_hat, axis=-1, keepdims=True) - xhat * inner) * rstd
    g_out[...] = g
    return g


def mlp_backward(last, scal, *refs):
    count = 1 if last else 5
    res, refs = refs[:count], refs[count:]
    (up, down, slope), refs = refs[:3], refs[3:]
    if last:
        low_out, d_hidden_out, small, mine, other, total = refs
        g = res[0][...]
        small[...] = jnp.zeros_like(small)
    else:
        g_out, low_out, d_hidden_out, small, mine, other, total = refs
        small[...] = jnp.zeros_like(small)
        g = norm_backward(scal, res, g_out, small)
    small[2:3, :] = jnp.sum(g, axis=0, keepdims=True)
    g_low = g.astype(BF16)
    low_out[...] = g_low
    d_hidden = (dot_abt(g_low, down[...]) * slope[...]).astype(BF16)
    d_hidden_out[...] = d_hidden
    small[3:4, :] = jnp.sum(d_hidden.astype(F32), axis=0, keepdims=True)
    total[...] = dot_abt(d_hidden, up[...])
    take_halves(scal, total, mine, other)


def attn_backward(scal, *refs):
    res, refs = refs[:5], refs[5:]
    (w, q_ref, k_ref, v_ref, soft_ref), refs = refs[:5], refs[5:]
    g_out, low_out, d_qkv_out, small, mine, other, total = refs
    small[...] = jnp.zeros_like(small)
    g = norm_backward(scal, res, g_out, small)
    small[2:3, :] = jnp.sum(g, axis=0, keepdims=True)
    g_low = g.astype(BF16)
    low_out[...] = g_low
    q, k, v = q_ref[...], k_ref[...], v_ref[...]
    width = q.shape[1]
    heads = head_mask(width)
    d_context = dot_ab(g_low, w[:, 3 * width :]).astype(BF16)
    d_q = jnp.zeros(q.shape, F32)
    d_k = jnp.zeros(q.shape, F32)
    d_v = jnp.zeros(q.shape, F32)
    for h in range(width // HEAD):
        soft = soft_ref[h]
        d_here = only(heads == h, d_context)
        d_soft = dot_abt(d_here, v)
        d_v = d_v + dot_atb(soft.astype(BF16), d_here)
        weighted = soft * d_soft
        delta = jnp.sum(weighted, axis=-1, keepdims=True)
        d_scores = (weighted - soft * delta).astype(BF16)
        d_q = d_q + dot_ab(d_scores, only(heads == h, k))
        d_k = d_k + dot_atb(d_scores, only(heads == h, q))
    d_q = (d_q * HEAD ** (-0.5)).astype(BF16)
    d_k = (d_k * HEAD ** (-0.5)).astype(BF16)
    d_v = d_v.astype(BF16)
    small[3:4, :width] = jnp.sum(d_q.astype(F32), axis=0, keepdims=True)
    small[4:5, :width] = jnp.sum(d_v.astype(F32), axis=0, keepdims=True)
    d_qkv = jnp.concatenate([d_q, d_k, d_v], axis=1)
    d_qkv_out[...] = d_qkv
    total[...] = dot_abt(d_qkv, w[:, : 3 * width])
    take_halves(scal, total, mine, other)


def input_backward(scal, *refs):
    res, (g_out, small) = refs[:5], refs[5:]
    small[...] = jnp.zeros_like(small)
    norm_backward(scal, res, g_out, small)


def row_halves(scal, full, outs):
    if len(outs) == 1:
        outs[0][...] = full[...].astype(BF16)
        return
    own, peer = outs
    half = own.shape[0]
    dp = scal[1]
    own[...] = full[pl.ds(pl.multiple_of(dp * half, half), half), :].astype(BF16)
    peer[...] = full[pl.ds(pl.multiple_of((1 - dp) * half, half), half), :].astype(BF16)


def column_halves(scal, full, outs):
    if len(outs) == 1:
        outs[0][...] = full[...].astype(BF16)
        return
    own, peer = outs
    half = own.shape[1]
    dp = scal[1]
    own[...] = full[:, pl.ds(pl.multiple_of(dp * half, 128), half)].astype(BF16)
    peer[...] = full[:, pl.ds(pl.multiple_of((1 - dp) * half, 128), half)].astype(BF16)


def mlp_weights(count, scal, low, d_hidden, active, g_low, *refs):
    full = refs[-1]
    full[...] = dot_atb(low[...], d_hidden[...])
    row_halves(scal, full, refs[:count])
    full[...] = dot_atb(active[...], g_low[...])
    column_halves(scal, full, refs[count : 2 * count])


def attn_weights(count, scal, low, d_qkv, context, g_low, *refs):
    full = refs[-1]
    width = context.shape[1]
    full[:, : 3 * width] = dot_atb(low[...], d_qkv[...])
    full[:, 3 * width :] = dot_atb(g_low[...], context[...])
    row_halves(scal, full, refs[:count])


def call(body, name, operands, outs, scratch=(), flops=0):
    out_shapes = [jax.ShapeDtypeStruct(s, d) for s, d in outs]
    moved = sum(o.size * o.dtype.itemsize for o in operands) + sum(
        o.size * o.dtype.itemsize for o in out_shapes
    )
    vmem = pl.BlockSpec(memory_space=pltpu.VMEM)
    return pl.pallas_call(
        body,
        out_shape=out_shapes,
        in_specs=[pl.BlockSpec(memory_space=pltpu.SMEM)] + [vmem] * (len(operands) - 1),
        out_specs=[vmem] * len(out_shapes),
        scratch_shapes=[pltpu.VMEM(s, d) for s, d in scratch],
        compiler_params=pltpu.CompilerParams(vmem_limit_bytes=VMEM_LIMIT),
        cost_estimate=pl.CostEstimate(flops=flops, bytes_accessed=moved, transcendentals=0),
        name=name,
    )(*operands)


def pairs_xor(axis, bit):
    return [(i, i ^ bit) for i in range(lax.axis_size(axis))]


def finish_sum(mine, other):
    near = mine + lax.ppermute(other, "tensor", pairs_xor("tensor", 1))
    total = near + lax.ppermute(near, "tensor", pairs_xor("tensor", 2))
    return total, lax.ppermute(total, "tensor", pairs_xor("tensor", 1))


def section_sum(part):
    section = lax.axis_index("section")
    inner = (section == 1) | (section == 2)
    near = part + lax.ppermute(part, "section", [(0, 1), (3, 2)])
    total = near + lax.ppermute(near, "section", [(1, 2), (2, 1)])
    back = lax.ppermute(total, "section", [(1, 0), (2, 3)])
    return jnp.where(inner, total, back)


def gathered(shard, axis, dp_count, parity):
    if dp_count != 2:
        return (lax.all_gather(shard, "dp", axis=axis, tiled=True),)
    part = shard.shape[0] // 2
    send = lax.dynamic_slice_in_dim(shard, parity * part, part, 0)
    near = lax.ppermute(send, "dp", pairs_xor("dp", 1))
    far = lax.ppermute(near, "section", pairs_xor("section", 1))
    return (shard, near, far)


def scattered(parts, axis):
    if len(parts) == 1:
        return lax.psum_scatter(parts[0], "dp", scatter_dimension=axis, tiled=True)
    own, peer = parts
    return own + lax.ppermute(peer, "dp", pairs_xor("dp", 1))


def shards(
    inputs,
    segments,
    cotangent,
    norm_gain,
    norm_shift,
    out_bias,
    attn_qkv,
    attn_out,
    attn_bias,
    mlp_in,
    mlp_out,
    mlp_bias,
):
    section = lax.axis_index("section")
    dp = lax.axis_index("dp")
    tensor = lax.axis_index("tensor")
    dp_count = lax.axis_size("dp")
    parity = section % 2
    layers = attn_qkv.shape[0]
    rows, model = inputs.shape[2], inputs.shape[3]
    half = rows // 2
    shard_rows = attn_qkv.shape[1]
    width = attn_out.shape[2]
    units = mlp_in.shape[2]
    heads = width // HEAD
    scal = jnp.stack([tensor % 2, dp, parity]).astype(jnp.int32)
    pieces = 3 if dp_count == 2 else 1

    attn_w, up_w, down_w = [], [], []
    for layer in range(layers):
        pack = jnp.concatenate(
            [attn_qkv[layer].reshape(shard_rows, 3 * width), attn_out[layer]], axis=1
        ).astype(BF16)
        attn_w.append(gathered(pack, 0, dp_count, parity))
        up_w.append(gathered(mlp_in[layer].astype(BF16), 0, dp_count, parity))
        down_w.append(gathered(mlp_out[layer].astype(BF16), 1, dp_count, parity))

    table = jnp.concatenate([norm_gain, norm_shift, out_bias], axis=0)
    table = lax.all_gather(table, "section", axis=0)
    gains = [table[s, 0:1] for s in range(2 * layers)]
    shifts = [table[s, 1:2] for s in range(2 * layers)]
    biases = [table[s, 2:3] for s in range(2 * layers)]
    seg = lax.dynamic_index_in_dim(segments[:, 0], section, 0, keepdims=False)
    seg_col, seg_row = seg[:, None], seg[None, :]

    row_f32 = ((rows, model), F32)
    row_low = ((rows, model), BF16)
    half_low = ((half, model), BF16)
    head_low = ((rows, width), BF16)
    full_scratch = [((rows, model), F32)]
    small_out = ((8, model), F32)

    kept = []
    res = [inputs.reshape(rows, model)]
    for layer in range(layers):
        s = 2 * layer
        out = call(
            functools.partial(attn_forward, layer == 0, pieces),
            "attn_forward",
            [scal, *res, gains[s], shifts[s], seg_col, seg_row, attn_bias[layer], *attn_w[layer]],
            [row_f32, row_low, ((model, 4 * width), BF16), head_low, head_low, head_low]
            + [((heads, rows, rows), F32), head_low, half_low, half_low],
            full_scratch,
            flops=2 * rows * model * 4 * width + 4 * heads * rows * rows * 256,
        )
        kept.append(out[:-2])
        res = [out[0], *finish_sum(*out[-2:]), biases[s]]
        s += 1
        out = call(
            functools.partial(mlp_forward, pieces),
            "mlp_forward",
            [scal, *res, gains[s], shifts[s], mlp_bias[layer][None], *up_w[layer], *down_w[layer]],
            [row_f32, row_low, ((model, units), BF16), ((units, model), BF16)]
            + [((rows, units), BF16), ((rows, units), F32), half_low, half_low],
            full_scratch,
            flops=4 * rows * model * units,
        )
        kept.append(out[:-2])
        res = [out[0], *finish_sum(*out[-2:]), biases[s]]

    core = tensor % 2
    x_last, mine, other, bias = res
    first_half = jnp.where(core == 0, mine, other).astype(F32)
    second_half = jnp.where(core == 0, other, mine).astype(F32)
    finished = x_last + jnp.concatenate([first_half, second_half], axis=0) + bias

    count = 2 if dp_count == 2 else 1
    attn_grads, up_grads, down_grads = [None] * layers, [None] * layers, [None] * layers
    smalls = []
    res = [cotangent.reshape(rows, model)]
    for layer in reversed(range(layers)):
        last = layer == layers - 1
        s = 2 * layer + 1
        x, low, up, down, active, slope = kept[s]
        out = call(
            functools.partial(mlp_backward, last),
            "mlp_backward",
            [scal, *res, up, down, slope],
            ([] if last else [row_f32])
            + [row_low, ((rows, units), BF16), small_out, half_low, half_low],
            full_scratch,
            flops=4 * rows * model * units,
        )
        g = res[0] if last else out[0]
        g_low, d_hidden, small, mine, other = out[-5:]
        smalls.append(small)
        res = [g, *finish_sum(mine, other), x, gains[s]]
        up_shape = ((shard_rows if count == 2 else model, units), BF16)
        down_shape = ((units, shard_rows if count == 2 else model), BF16)
        parts = call(
            functools.partial(mlp_weights, count),
            "mlp_weights",
            [scal, low, d_hidden, active, g_low],
            [up_shape] * count + [down_shape] * count,
            [((model, units), F32)],
            flops=4 * rows * model * units,
        )
        up_grads[layer] = section_sum(scattered(parts[:count], 0))
        down_grads[layer] = section_sum(scattered(parts[count:], 1))
        s -= 1
        x, low, w, q, k, v, soft, context = kept[s]
        g, g_low, d_qkv, small, mine, other = call(
            attn_backward,
            "attn_backward",
            [scal, *res, w, q, k, v, soft],
            [row_f32, row_low, ((rows, 3 * width), BF16), small_out, half_low, half_low],
            full_scratch,
            flops=2 * rows * model * 4 * width + 10 * heads * rows * rows * 256,
        )
        smalls.append(small)
        res = [g, *finish_sum(mine, other), x, gains[s]]
        parts = call(
            functools.partial(attn_weights, count),
            "attn_weights",
            [scal, low, d_qkv, context, g_low],
            [((shard_rows if count == 2 else model, 4 * width), BF16)] * count,
            [((model, 4 * width), F32)],
            flops=2 * rows * model * 4 * width,
        )
        attn_grads[layer] = section_sum(scattered(parts, 0))
    input_grad, small = call(input_backward, "input_backward", [scal, *res], [row_f32, small_out])
    smalls.append(small)

    small = jnp.stack(smalls)
    if dp_count == 2:
        small = section_sum(small + lax.ppermute(small, "dp", pairs_xor("dp", 1)))
    else:
        small = lax.psum(small, ("section", "dp"))
    gain_rows = small[1:, 0][::-1]
    shift_rows = small[1:, 1][::-1]
    bias_rows = small[:-1, 2][::-1]
    mlp_rows = jnp.stack([small[2 * (layers - 1 - l), 3, :units] for l in range(layers)])
    attn_rows = jnp.stack([small[2 * (layers - 1 - l) + 1, 3:5, :width] for l in range(layers)])

    def own(rows_all):
        return lax.dynamic_slice_in_dim(rows_all, section, 1, 0)

    pack = jnp.stack(attn_grads)
    return (
        finished.reshape(inputs.shape),
        input_grad.reshape(inputs.shape),
        own(gain_rows),
        own(shift_rows),
        own(bias_rows),
        pack[:, :, : 3 * width].reshape(layers, shard_rows, 3, width).astype(F32),
        pack[:, :, 3 * width :].astype(F32),
        attn_rows,
        jnp.stack(up_grads).astype(F32),
        jnp.stack(down_grads).astype(F32),
        mlp_rows,
    )


def solution(mesh):
    placed = (
        P("section", "dp", None, None),
        P(None, "dp", None),
        P("section", "dp", None, None),
        P("section", None),
        P("section", None),
        P("section", None),
        P(None, "dp", None, "tensor"),
        P(None, "dp", "tensor"),
        P(None, None, "tensor"),
        P(None, "dp", "tensor"),
        P(None, "tensor", "dp"),
        P(None, "tensor"),
    )
    return jax.shard_map(
        shards,
        mesh=mesh,
        in_specs=placed,
        out_specs=(
            P("section", "dp", None, None),
            P("section", "dp", None, None),
            P("section", None),
            P("section", None),
            P("section", None),
            P(None, "dp", None, "tensor"),
            P(None, "dp", "tensor"),
            P(None, None, "tensor"),
            P(None, "dp", "tensor"),
            P(None, "tensor", "dp"),
            P(None, "tensor"),
        ),
        check_vma=False,
    )
```

```python
import functools

import jax
import jax.numpy as jnp
from jax import lax
from jax.experimental import pallas as pl
from jax.experimental.pallas import tpu as pltpu
from jax.sharding import PartitionSpec as P

HEAD = 64
EPS = 1e-06
MASKED = -1e30
BF16 = jnp.bfloat16
F32 = jnp.float32
VMEM_LIMIT = 12 * 1024 * 1024
SIDE = ("shuttle", "attn_pack", "mlp_pack")
TINY = ("add", "emit")
SIDE_COST, MAIN_COST, TINY_COST = 3000000000, 1000, 1000


def dot_ab(a, b):
    return lax.dot_general(a, b, (((1,), (0,)), ((), ())), preferred_element_type=F32)


def dot_abt(a, b):
    return lax.dot_general(a, b, (((1,), (1,)), ((), ())), preferred_element_type=F32)


def dot_atb(a, b):
    return lax.dot_general(a, b, (((0,), (0,)), ((), ())), preferred_element_type=F32)


FORE = -1
MOVES = (
    ((), (), ()),
    ((0,), (FORE,), (FORE,)),
    ((1, 0), (FORE, 2), (1,)),
    ((0,), (3, 2, 1), (4,)),
    (("down", 1, 0), 3, 2, ("up", 1, 1), 5, 4, 3, ("attn", 1, 2), 6, 5, 6, 4, ("down", 0, 3), 6, 5)
    + (("up", 0, 4), ("attn", 0, 5)),
)
SPLIT_ATTN, SPLIT_MLP = (1, 1), (1, 1)


def span(start, size):
    return pl.ds(pl.multiple_of(start, size), size)


class Copies:
    def __init__(self, sems):
        self.sems, self.used = sems, 0

    def __call__(self, src, dst):
        copy = pltpu.make_async_copy(src, dst, self.sems.at[self.used])
        self.used += 1
        copy.start()
        return copy

    def all(self, pairs):
        return [self(src, dst) for src, dst in pairs]


def wait(*copies):
    for copy in copies:
        copy.wait()


def normalized(x):
    center = x - jnp.mean(x, axis=-1, keepdims=True)
    rstd = lax.rsqrt(jnp.mean(center * center, axis=-1, keepdims=True) + EPS)
    return center * rstd, rstd


def norm_rows(scal, table, sub_layer):
    return table[jnp.bitwise_xor(scal[3], sub_layer)]


def put_halves(scal, dst, mine, other):
    half = mine.shape[0]
    core = scal[0]
    dst[span(core * half, half), :] = mine[...].astype(F32)
    dst[span((1 - core) * half, half), :] = other[...].astype(F32)


def take_halves(scal, src, mine, other):
    half = mine.shape[0]
    core = scal[0]
    mine[...] = src[span(core * half, half), :].astype(BF16)
    other[...] = src[span((1 - core) * half, half), :].astype(BF16)


def attn_pieces(scal, pieces, dst):
    if len(pieces) == 1:
        return [(pieces[0], dst)]
    own, near, far, direct = pieces
    half, part = own.shape[1], near.shape[0]
    dp, parity = scal[1], scal[2]
    peer = span((1 - dp) * half, half)
    return [
        (own, dst.at[:, span(dp * half, half)]),
        (near, dst.at[span(parity * part, part), peer]),
        (far, dst.at[span((1 - parity) * part, part), peer]),
        (direct, dst.at[pl.ds(2 * part, part), peer]),
    ]


def mlp_pieces(scal, pieces, up, down):
    if len(pieces) == 2:
        return [(pieces[0], up)], [(pieces[1], down)]
    own_up, own_down, near, far, direct = pieces
    half, part = own_up.shape[0], near.shape[0] // 2
    dp, parity = scal[1], scal[2]
    peer = span((1 - dp) * half, half)
    ups = [(own_up, up.at[span(dp * half, half), :])]
    downs = [(own_down, down.at[:, span(dp * half, half)])]
    for piece, index in ((near, parity), (far, 1 - parity), (direct, 2)):
        ups.append(
            (piece.at[pl.ds(0, part), :], up.at[span((1 - dp) * half + index * part, part), :])
        )
        for side in (0, 1):
            downs.append(
                (
                    piece.at[pl.ds(part, part), pl.ds(side * half, half)],
                    down.at[span((2 * index + side) * part, part), peer],
                )
            )
    return ups, downs


def head_mask(width):
    return lax.broadcasted_iota(jnp.int32, (1, width), 1) // HEAD


def only(mask, values):
    return jnp.where(mask, values, jnp.zeros((), values.dtype))


def attn_pack(layer, scal, qkv, out, own, shared, direct, wide, low, sems):
    copy = Copies(sems)
    part = shared.shape[0]
    count = qkv.shape[1]
    rest = count - 2 * part
    loads = []
    for index in (scal[2], 1 - scal[2]):
        here = span(index * part, part)
        loads.append((here, [copy(qkv.at[layer, here], wide.at[here])]))
    loads.append(
        (
            pl.ds(2 * part, part),
            [
                copy(qkv.at[layer, pl.ds(2 * part, rest)], wide.at[pl.ds(2 * part, rest)]),
                copy(out.at[layer], wide.at[pl.ds(count, part - rest)]),
            ],
        )
    )
    keep = []
    for (here, copies), piece in zip(loads, (shared, None, direct)):
        wait(*copies)
        third = wide[here, :].astype(BF16)
        low[here, :] = third
        if piece is not None:
            piece[...] = third
        keep.append(copy(low.at[here], own.at[here]))
    wait(*keep)


def mlp_pack(
    layer, scal, up, down, own_up, own_down, shared, direct, wide_up, wide_down, low_up, low_down,
    sems,
):
    copy = Copies(sems)
    half, part = wide_up.shape[0], shared.shape[0] // 2
    loads = []
    for index in (scal[2], 1 - scal[2], 2):
        here, there = span(index * part, part), span(2 * index * part, 2 * part)
        loads.append(
            (
                here,
                there,
                copy(up.at[layer, here], wide_up.at[here]),
                copy(down.at[layer, there], wide_down.at[there]),
            )
        )
    keep = []
    for (here, there, *copies), piece in zip(loads, (shared, None, direct)):
        wait(*copies)
        third_up, third_down = wide_up[here, :].astype(BF16), wide_down[there, :].astype(BF16)
        low_up[here, :] = third_up
        low_down[there, :] = third_down
        keep.append(copy(low_up.at[here], own_up.at[here]))
        keep.append(copy(low_down.at[there], own_down.at[there]))
        if piece is not None:
            piece[:part, :] = third_up
            piece[part:, :half] = third_down[:part]
            piece[part:, half:] = third_down[part:]
    wait(*keep)


def residual(scal, table, sub_layer, refs, x_out):
    x_prev, mine, other = refs
    put_halves(scal, x_out, mine, other)
    bias = norm_rows(scal, table, sub_layer - 1)[2:3]
    x_out[...] = x_prev[...] + (x_out[...] + bias)
    return x_out[...]


def attn_forward(sub_layer, scal, table, *refs):
    if sub_layer == 0:
        x_ref, refs = refs[0], refs[1:]
    else:
        res, refs = refs[:3], refs[3:]
    (seg_col, seg_row, inner, w), refs = refs[:4], refs[4:]
    if sub_layer:
        x_ref, refs = refs[0], refs[1:]
        residual(scal, table, sub_layer, res, x_ref)
    low_out, qkv_out, soft_out, ctx_out, mine, other, total = refs
    x = x_ref[...]
    xhat, _ = normalized(x)
    norm = norm_rows(scal, table, sub_layer)
    low = (xhat * norm[0:1] + norm[1:2]).astype(BF16)
    low_out[...] = low
    width = ctx_out.shape[1]
    q = (dot_abt(low, w[:width]) + inner[0:1, :]).astype(BF16)
    k = dot_abt(low, w[width : 2 * width]).astype(BF16)
    v = (dot_abt(low, w[2 * width : 3 * width]) + inner[1:2, :]).astype(BF16)
    qkv_out[0] = q
    qkv_out[1] = k
    qkv_out[2] = v
    same = seg_col[...] == seg_row[...]
    heads = head_mask(width)
    context = jnp.zeros((x.shape[0], width), F32)
    for h in range(width // HEAD):
        scores = dot_abt(only(heads == h, q), k) * HEAD ** (-0.5)
        scores = jnp.where(same, scores, MASKED)
        expanded = jnp.exp(scores - jnp.max(scores, axis=-1, keepdims=True))
        soft = expanded / jnp.sum(expanded, axis=-1, keepdims=True)
        soft_out[h] = soft
        context = context + dot_ab(soft.astype(BF16), only(heads == h, v))
    context = context.astype(BF16)
    ctx_out[...] = context
    total[...] = dot_ab(context, w[3 * width :])
    take_halves(scal, total, mine, other)


def mlp_forward(sub_layer, count, scal, table, *refs):
    res, up_bias, up, down, refs = refs[:3], refs[3], refs[4], refs[5], refs[6:]
    if count:
        cotangent, refs = refs[0], refs[1:]
        x_out, mine, other, small, back_mine, back_other = refs[:6]
        grads, (total, full) = refs[6:-2], refs[-2:]
    else:
        x_out, low_out, active_out, slope_out, mine, other, total = refs
    x = residual(scal, table, sub_layer, res, x_out)
    xhat, _ = normalized(x)
    norm = norm_rows(scal, table, sub_layer)
    low = (xhat * norm[0:1] + norm[1:2]).astype(BF16)
    hidden = dot_ab(low, up[...]) + up_bias[...]
    phi = 0.5 * (1.0 + lax.erf(hidden * 0.7071067811865476))
    slope = phi + hidden * (0.3989422804014327 * jnp.exp(-0.5 * hidden * hidden))
    active = (hidden * phi).astype(BF16)
    if count:
        small[...] = jnp.zeros_like(small)
        mlp_back_part(
            scal, count, cotangent[...], low, active, up, down, slope, small, back_mine, back_other,
            grads, total, full,
        )
    else:
        low_out[...] = low
        active_out[...] = active
        slope_out[...] = slope
    total[...] = dot_ab(active, down[...])
    take_halves(scal, total, mine, other)


def norm_backward(scal, table, sub_layer, g_prev, mine, other, x, g_out, small):
    put_halves(scal, g_out, mine, other)
    d_normed = g_out[...]
    xhat, rstd = normalized(x[...])
    small[0:1, :] = jnp.sum(d_normed * xhat, axis=0, keepdims=True)
    small[1:2, :] = jnp.sum(d_normed, axis=0, keepdims=True)
    d_hat = d_normed * norm_rows(scal, table, sub_layer)[0:1]
    inner = jnp.mean(d_hat * xhat, axis=-1, keepdims=True)
    g = g_prev[...] + (d_hat - jnp.mean(d_hat, axis=-1, keepdims=True) - xhat * inner) * rstd
    g_out[...] = g
    return g


def mlp_back_part(
    scal, count, g, low, active, up, down, slope, small, mine, other, grads, total, full
):
    small[2:3, :] = jnp.sum(g, axis=0, keepdims=True)
    g_low = g.astype(BF16)
    full[...] = dot_atb(active, g_low)
    column_halves(scal, full, grads[: len(grads) // 2])
    d_hidden = (dot_abt(g_low, down[...]) * slope).astype(BF16)
    small[3:4, :] = jnp.sum(d_hidden.astype(F32), axis=0, keepdims=True)
    total[...] = dot_abt(d_hidden, up[...])
    take_halves(scal, total, mine, other)
    full[...] = dot_atb(low, d_hidden)
    row_halves(scal, full, grads[len(grads) // 2 :])


def mlp_backward(sub_layer, scal, table, *refs):
    res, (low, active, slope, up, down), refs = refs[:4], refs[4:9], refs[9:]
    g_out, small, mine, other = refs[:4]
    grads, (total, full) = refs[4:-2], refs[-2:]
    small[...] = jnp.zeros_like(small)
    g = norm_backward(scal, table, sub_layer + 1, *res, g_out, small)
    mlp_back_part(
        scal, 0, g, low[...], active[...], up, down, slope[...], small, mine, other, grads, total,
        full,
    )


def attn_backward(sub_layer, scal, table, *refs):
    res, (low, qkv, soft_all, ctx, w), refs = refs[:4], refs[4:9], refs[9:]
    g_out, small, mine, other = refs[:4]
    grads, (total, full) = refs[4:-2], refs[-2:]
    small[...] = jnp.zeros_like(small)
    g = norm_backward(scal, table, sub_layer + 1, *res, g_out, small)
    small[2:3, :] = jnp.sum(g, axis=0, keepdims=True)
    g_low = g.astype(BF16)
    q, k, v = qkv[0], qkv[1], qkv[2]
    width = q.shape[1]
    heads = head_mask(width)
    d_context = dot_abt(g_low, w[3 * width :]).astype(BF16)
    d_q = jnp.zeros(q.shape, F32)
    d_k = jnp.zeros(q.shape, F32)
    d_v = jnp.zeros(q.shape, F32)
    for h in range(width // HEAD):
        soft = soft_all[h]
        d_here = only(heads == h, d_context)
        d_soft = dot_abt(d_here, v)
        d_v = d_v + dot_atb(soft.astype(BF16), d_here)
        weighted = soft * d_soft
        delta = jnp.sum(weighted, axis=-1, keepdims=True)
        d_scores = (weighted - soft * delta).astype(BF16)
        d_q = d_q + dot_ab(d_scores, only(heads == h, k))
        d_k = d_k + dot_atb(d_scores, only(heads == h, q))
    d_q = (d_q * HEAD ** (-0.5)).astype(BF16)
    d_k = (d_k * HEAD ** (-0.5)).astype(BF16)
    d_v = d_v.astype(BF16)
    small[3:4, :width] = jnp.sum(d_q.astype(F32), axis=0, keepdims=True)
    small[4:5, :width] = jnp.sum(d_v.astype(F32), axis=0, keepdims=True)
    total[...] = (
        dot_ab(d_q, w[:width])
        + dot_ab(d_k, w[width : 2 * width])
        + dot_ab(d_v, w[2 * width : 3 * width])
    )
    take_halves(scal, total, mine, other)
    for index, part in enumerate((d_q, d_k, d_v)):
        full[index * width : (index + 1) * width, :] = dot_atb(part, low[...])
    full[3 * width :, :] = dot_atb(ctx[...], g_low)
    column_halves(scal, full, grads)


def finish(last, scal, table, *refs):
    g_prev, mine, other, x, x_last, fore_mine, fore_other = refs[:7]
    g_hbm, out_hbm, small, g_out, out, sems = refs[7:]
    copy = Copies(sems)
    small[...] = jnp.zeros_like(small)
    residual(scal, table, last, (x_last, fore_mine, fore_other), out)
    keep = [copy(out, out_hbm)]
    norm_backward(scal, table, 0, g_prev, mine, other, x, g_out, small)
    keep.append(copy(g_out, g_hbm))
    wait(*keep)


def column_halves(scal, full, outs):
    if len(outs) == 1:
        outs[0][...] = full[...].astype(BF16)
        return
    count = len(outs) // 2
    rows, half = outs[0].shape
    for index in range(count):
        own, peer = outs[2 * index], outs[2 * index + 1]
        here = slice(index * rows, (index + 1) * rows)
        own[...] = full[here, span(scal[1] * half, half)].astype(BF16)
        peer[...] = full[here, span((1 - scal[1]) * half, half)].astype(BF16)


def row_halves(scal, full, outs):
    if len(outs) == 1:
        outs[0][...] = full[...].astype(BF16)
        return
    rows = outs[0].shape[0]
    count = len(outs) // 2
    for index in range(count):
        own, peer = scal[1] * count + index, (1 - scal[1]) * count + index
        outs[2 * index][...] = full[span(own * rows, rows), :].astype(BF16)
        outs[2 * index + 1][...] = full[span(peer * rows, rows), :].astype(BF16)


def add_kernel(held, sent, out):
    out[...] = held[...] + sent[...]


def emit_sums(layer, count, aliased, scal, *refs):
    blocks, refs = refs[: 2 * count], refs[2 * count + aliased :]
    *outs, wide, sems = refs
    inner = (scal[3] == 1) | (scal[3] == 2)
    rows = blocks[0].shape[0]
    for index in range(count):
        held, sent = blocks[2 * index], blocks[2 * index + 1]
        here = slice(index * rows, (index + 1) * rows)

        @pl.when(inner)
        def _():
            wide[here, :] = held[...].astype(F32)

        @pl.when(jnp.logical_not(inner))
        def _():
            wide[here, :] = sent[...].astype(F32)

    copy = Copies(sems)
    copies, row = [], 0
    for out in outs:
        copies.append(copy(wide.at[pl.ds(row, out.shape[1])], out.at[layer]))
        row += out.shape[1]
    wait(*copies)


def shuttle(plan, count, scal, *refs):
    refs, sems = refs[:-1], refs[-1]
    copy = Copies(sems)
    wait(*[copy(src, dst) for src, dst in plan(scal, refs[:count], refs[count:])])


SPACES = {"H": pltpu.HBM, "V": pltpu.VMEM, "W": pltpu.VMEM, "S": pltpu.SMEM}


def call(body, name, operands, outs, scratch=(), copies=0, aliases=None):
    def shape_of(shape, dtype, place):
        return jax.ShapeDtypeStruct(shape, dtype) if place == "W" else SPACES[place](shape, dtype)

    sems = [pltpu.SemaphoreType.DMA((copies,))] if copies else []
    return pl.pallas_call(
        body,
        out_shape=[shape_of(*out) for out in outs],
        in_specs=[pl.BlockSpec(memory_space=SPACES[place]) for _, place in operands],
        out_specs=[pl.BlockSpec(memory_space=SPACES[place]) for _, _, place in outs],
        scratch_shapes=[pltpu.VMEM(s, d) for s, d in scratch] + sems,
        input_output_aliases=aliases or {},
        compiler_params=pltpu.CompilerParams(vmem_limit_bytes=VMEM_LIMIT),
        cost_estimate=pl.CostEstimate(
            flops=SIDE_COST if name in SIDE else TINY_COST if name in TINY else MAIN_COST,
            bytes_accessed=1000,
            transcendentals=0,
        ),
        name=name,
    )(
        *[
            pltpu.with_memory_space_constraint(array, pltpu.HBM) if place == "H" else array
            for array, place in operands
        ]
    )


def pairs_xor(axis, bit):
    return [(i, i ^ bit) for i in range(lax.axis_size(axis))]


class Order:
    def __init__(self):
        self.token = None

    def __call__(self, *arrays):
        if self.token is None:
            return arrays
        held = lax.optimization_barrier(tuple(arrays) + (self.token,))
        return held[:-1]

    def hold(self, *arrays):
        held = lax.optimization_barrier(tuple(arrays) + (self.token,))
        self.token = held[-1]
        return held[:-1]

    def run(self, body, name, operands, *args, **kwargs):
        arrays = self(*[array for array, _ in operands])
        places = [place for _, place in operands]
        out = call(body, name, list(zip(arrays, places)), *args, **kwargs)
        self.token = out[-1]
        return out


def near_sum(order, mine, arrived):
    mine, arrived = order(mine, arrived)
    near = mine + arrived
    order.token = near
    return near


class Block:
    def __init__(self, order, own, peer, routes):
        self.order, self.held, self.routes = order, own, list(routes)
        self.sent = lax.ppermute(peer, "dp", pairs_xor("dp", 1))

    def step(self):
        [self.held] = self.order.run(
            add_kernel,
            "add",
            [(self.held, "W"), (self.sent, "W")],
            [(self.held.shape, self.held.dtype, "W")],
        )
        if self.routes:
            self.sent = lax.ppermute(self.held, "section", self.routes.pop(0))


LINE = ([(0, 1), (3, 2)], [(1, 2), (2, 1)], [(1, 0), (2, 3)])


def shards(
    inputs,
    segments,
    cotangent,
    norm_gain,
    norm_shift,
    out_bias,
    attn_qkv,
    attn_out,
    attn_bias,
    mlp_in,
    mlp_out,
    mlp_bias,
):
    section = lax.axis_index("section")
    dp = lax.axis_index("dp")
    tensor = lax.axis_index("tensor")
    dp_count = lax.axis_size("dp")
    layers = attn_qkv.shape[0]
    rows, model = inputs.shape[2], inputs.shape[3]
    half = rows // 2
    shard = attn_qkv.shape[1]
    width = attn_out.shape[2]
    units = mlp_in.shape[2]
    heads = width // HEAD
    core = tensor % 2
    scal = (jnp.stack([core, dp, section % 2, section]).astype(jnp.int32), "S")
    paired = dp_count == 2
    order = Order()

    def places(place, arrays):
        return [(array, place) for array in arrays]

    table = jnp.concatenate([norm_gain, norm_shift, out_bias], axis=0)
    table = jnp.pad(table, ((0, 5), (0, 0)))[None]
    for bit in (1, 2):
        table = jnp.concatenate([table, lax.ppermute(table, "section", pairs_xor("section", bit))])
    table = (table, "V")

    qkv_t = attn_qkv.transpose(0, 2, 3, 1).reshape(layers, 3 * width, shard)
    out_t = attn_out.transpose(0, 2, 1)

    def sent(shared, direct):
        near = lax.ppermute(shared, "dp", pairs_xor("dp", 1))
        return [near, None, lax.ppermute(direct, "dp", pairs_xor("dp", 1))]

    def send_on(weights):
        if paired:
            [weights[-3]] = order.hold(weights[-3])
            weights[-2] = lax.ppermute(weights[-3], "section", pairs_xor("section", 1))

    def arrived_by_now(weights, index):
        if paired:
            [weights[index]] = order.hold(weights[index])

    def attn_gather(layer):
        if not paired:
            pack = jnp.concatenate([qkv_t[layer], out_t[layer]], axis=0).astype(BF16)
            return [lax.all_gather(pack, "dp", axis=1, tiled=True)]
        third = 4 * width // 3
        own, shared, direct = order.run(
            functools.partial(attn_pack, layer),
            "attn_pack",
            [scal, (qkv_t, "H"), (out_t, "H")],
            [((4 * width, shard), BF16, "H")] + [((third, shard), BF16, "V")] * 2,
            [((4 * width, shard), F32), ((4 * width, shard), BF16)],
            copies=7,
        )
        return [own, *sent(shared, direct)]

    def mlp_gather(layer):
        if not paired:
            return [
                lax.all_gather(mlp_in[layer].astype(BF16), "dp", axis=0, tiled=True),
                lax.all_gather(mlp_out[layer].astype(BF16), "dp", axis=1, tiled=True),
            ]
        third = 2 * shard // 3
        own_up, own_down, shared, direct = order.run(
            functools.partial(mlp_pack, layer),
            "mlp_pack",
            [scal, (mlp_in, "H"), (mlp_out, "H")],
            [((shard, units), BF16, "H"), ((units, shard), BF16, "H")]
            + [((third, units), BF16, "V")] * 2,
            [(shape, kind) for kind in (F32, BF16) for shape in ((shard, units), (units, shard))],
            copies=12,
        )
        return [own_up, own_down, *sent(shared, direct)]

    seg = lax.dynamic_index_in_dim(segments[:, 0], section, 0, keepdims=False)
    segs = [(seg[:, None], "V"), (seg[None, :], "V")]

    row_f32, row_low = ((rows, model), F32), ((rows, model), BF16)
    unit_f32, unit_low = ((rows, units), F32), ((rows, units), BF16)
    half_low = ((half, model), BF16)
    small_out = ((8, model), F32, "W")
    qkv_low, soft_f32 = ((3, rows, width), BF16), ((heads, rows, rows), F32)
    ctx_low, attn_full = ((rows, width), BF16), ((4 * width, model), BF16)
    up_full, down_full = ((model, units), BF16), ((units, model), BF16)

    def held(*shapes):
        return [shape + ("V",) for shape in shapes]

    def move_data(save=(), fetch=(), attn=None, mlp=None):
        pieces = attn or mlp or []

        def plan(scal, ins, outs):
            count = len(save) + len(fetch)
            pairs = list(zip(ins[:count], outs[:count]))
            if attn:
                pairs += attn_pieces(scal, ins[count:], outs[count])
            if mlp:
                ups, downs = mlp_pieces(scal, ins[count:], *outs[count:])
                pairs += ups + downs
            return pairs

        outs = [(array.shape, array.dtype, "H") for array in save]
        outs += [(array.shape, array.dtype, "V") for array in fetch]
        outs += held(attn_full) if attn else held(up_full, down_full) if mlp else []
        operands = places("V", save) + places("H", list(fetch) + list(pieces))
        return order.run(
            functools.partial(shuttle, plan, len(operands)),
            "shuttle",
            [scal, *operands],
            outs,
            copies=len(save) + len(fetch) + (11 if mlp else 4),
        )

    def nothing():
        return None

    def tensor_sum(mine, other, window=nothing, ahead=nothing, moves=((), (), ())):
        arrived = lax.ppermute(other, "tensor", pairs_xor("tensor", 1))
        ahead()
        move(*moves[0])
        near = near_sum(order, mine, arrived)
        arrived = lax.ppermute(near, "tensor", pairs_xor("tensor", 2))
        window()
        move(*moves[1])
        total = near_sum(order, near, arrived)
        arrived = lax.ppermute(total, "tensor", pairs_xor("tensor", 1))
        move(*moves[2])
        return [total, arrived]

    def fore_steps(mine, other):
        arrived = lax.ppermute(other, "tensor", pairs_xor("tensor", 1))
        yield
        near = near_sum(order, mine, arrived)
        arrived = lax.ppermute(near, "tensor", pairs_xor("tensor", 2))
        yield
        total = near_sum(order, near, arrived)
        yield total, lax.ppermute(total, "tensor", pairs_xor("tensor", 1))

    def attn_step(s, res, w):
        return order.run(
            functools.partial(attn_forward, s),
            "attn_forward",
            [scal, table, *places("V", res), *segs, *places("V", [attn_bias[s // 2], w])],
            held(*([row_f32] if s else []), row_low, qkv_low, soft_f32, ctx_low, half_low, half_low),
            [row_f32],
        )

    def mlp_step(s, res, up, down, cotangent=None):
        last = cotangent is not None
        operands = [*res, mlp_bias[s // 2][None], up, down] + ([cotangent] if last else [])
        if last:
            grads = mlp_shapes(s // 2)
            outs = held(row_f32, half_low, half_low) + [small_out] + held(half_low, half_low)
            outs += grads
        else:
            grads = []
            outs = held(row_f32, row_low, unit_low, unit_f32, half_low, half_low)
        return order.run(
            functools.partial(mlp_forward, s, len(grads)),
            "mlp_forward",
            [scal, table, *places("V", operands)],
            outs,
            [row_f32] + ([(up_full[0], F32)] if last else []),
        )

    def mlp_shapes(layer):
        if not paired:
            return [(down_full[0], BF16, "W"), (up_full[0], BF16, "W")]
        splits = SPLIT_MLP[layer]
        down, up = (units // splits, shard), (shard // splits, units)
        return [(down, BF16, "W")] * (2 * splits) + [(up, BF16, "W")] * (2 * splits)

    def attn_shapes(layer):
        if not paired:
            return [(attn_full[0], BF16, "W")]
        splits = SPLIT_ATTN[layer]
        return [((4 * width // splits, shard), BF16, "W")] * (2 * splits)

    chunks = []

    def add_chunks(parts, axis):
        if not paired:
            whole = lax.psum_scatter(parts[0], "dp", scatter_dimension=axis, tiled=True)
            chunks.append(lax.psum(whole, "section"))
            return
        for own, peer in zip(parts[0::2], parts[1::2]):
            chunks.append(Block(order, own, peer, LINE))

    emitted = {}

    def emit(kind, layer, blocks):
        shape = {"up": (shard, units), "down": (units, shard), "attn": (4 * width, shard)}[kind]
        outs = [((layers,) + shape, F32, "H")]
        if kind == "attn":
            outs = [((layers, count, shard), F32, "H") for count in (3 * width, width)]
        before = emitted.get(kind, [])
        assert not any(block.routes for block in blocks)
        operands = [operand for block in blocks for operand in (block.held, block.sent)]
        emitted[kind] = order.run(
            functools.partial(emit_sums, layer, len(blocks), len(before)),
            "emit",
            [scal, *places("W", operands), *places("H", before)],
            outs,
            [(shape, F32)],
            copies=2,
            aliases={1 + len(operands) + index: index for index in range(len(before))},
        )

    def move(*indices):
        for index in indices:
            if index == FORE:
                fore.append(next(fore[0]))
            elif not paired:
                continue
            elif isinstance(index, tuple):
                kind, layer, *blocks = index
                emit(kind, layer, [chunks[block] for block in blocks])
            else:
                chunks[index].step()

    def mlp_chunks(parts):
        add_chunks(parts[: len(parts) // 2], 1)
        add_chunks(parts[len(parts) // 2 :], 0)

    def back(body, name, s, operands, full, grads):
        return order.run(
            functools.partial(body, s),
            name,
            [scal, table, *places("V", operands)],
            held(row_f32) + [small_out] + held(half_low, half_low) + grads,
            [row_f32, (full[0], F32)],
        )

    box = {}

    def keep(names, values):
        box.update(zip(names, values))

    def kept(*names):
        return [box[name] for name in names]

    x0 = inputs.reshape(rows, model)
    pieces = [attn_gather(0), mlp_gather(0)]
    send_on(pieces[0])
    pieces.append(attn_gather(1))
    [w] = move_data(attn=pieces[0])
    low, qkv, soft, ctx, *halves = attn_step(0, [x0], w)

    def ahead():
        send_on(pieces[1])

    def window():
        pieces.append(mlp_gather(1))
        keep(
            ("low0", "qkv0", "soft0", "ctx0", "up", "down"),
            move_data([low, qkv, soft, ctx], mlp=pieces[1]),
        )
        send_on(pieces[2])

    total = tensor_sum(*halves, window, ahead)
    x1, low, active, slope, *halves = mlp_step(1, [x0, *total], box["up"], box["down"])

    def ahead():
        arrived_by_now(pieces[2], -1)

    def window():
        keep(
            ("x1", "low1", "active1", "slope1", "w"),
            move_data([x1, low, active, slope], attn=pieces[2]),
        )
        send_on(pieces[3])

    total = tensor_sum(*halves, window, ahead)
    x2, low, qkv, soft, ctx, *halves = attn_step(2, [x1, *total], box["w"])

    def ahead():
        arrived_by_now(pieces[3], -1)

    def window():
        keep(
            ("x2", "low2", "qkv2", "soft2", "ctx2", "up", "down"),
            move_data([x2, low, qkv, soft, ctx], mlp=pieces[3]),
        )

    total = tensor_sum(*halves, window, ahead)
    g = cotangent.reshape(rows, model)
    x3, fore_mine, fore_other, small3, *rest = mlp_step(
        3, [x2, *total], box["up"], box["down"], g
    )
    fore = [fore_steps(fore_mine, fore_other)]

    def window():
        keep(
            ("low", "ctx", "qkv", "soft", "w"),
            move_data(fetch=kept("low2", "ctx2", "qkv2", "soft2"), attn=pieces[2]),
        )

    total = tensor_sum(*rest[:2], window, lambda: mlp_chunks(rest[2:]), MOVES[0])
    operands = [g, *total, x3, *kept("low", "qkv", "soft", "ctx", "w")]
    g, small2, *rest = back(
        attn_backward, "attn_backward", 2, operands, attn_full, attn_shapes(1)
    )

    def window():
        keep(
            ("x3", "x", "low", "active", "slope", "up", "down"),
            move_data([x3], kept("x2", "low1", "active1", "slope1"), mlp=pieces[1]),
        )

    total = tensor_sum(*rest[:2], window, lambda: add_chunks(rest[2:], 1), MOVES[1])
    operands = [g, *total, *kept("x", "low", "active", "slope", "up", "down")]
    g, small1, *rest = back(mlp_backward, "mlp_backward", 1, operands, up_full, mlp_shapes(0))

    def window():
        keep(
            ("x", "low", "ctx", "qkv", "soft", "w"),
            move_data(fetch=kept("x1", "low0", "ctx0", "qkv0", "soft0"), attn=pieces[0]),
        )

    total = tensor_sum(*rest[:2], window, lambda: mlp_chunks(rest[2:]), MOVES[2])
    operands = [g, *total, *kept("x", "low", "qkv", "soft", "ctx", "w")]
    g, small0, *rest = back(
        attn_backward, "attn_backward", 0, operands, attn_full, attn_shapes(0)
    )
    total = tensor_sum(*rest[:2], ahead=lambda: add_chunks(rest[2:], 1), moves=MOVES[3])
    while len(fore) < 4:
        move(FORE)
    input_grad, outputs, small = order.run(
        functools.partial(finish, 2 * layers),
        "finish",
        [scal, table, *places("V", [g, *total, x0, box["x3"], *fore[3]])],
        [row_f32 + ("H",), row_f32 + ("H",), small_out],
        [row_f32] * 2,
        copies=2,
    )

    small = jnp.stack([small3, small2, small1, small0, small])
    if paired:
        chunks.append(Block(order, small, small, [pairs_xor("section", 1), pairs_xor("section", 2)]))
        move(*MOVES[4])
        small = chunks[-1].held
        [up_grad], [down_grad], (qkv_grad, out_grad) = (emitted[k] for k in ("up", "down", "attn"))
    else:
        small = lax.psum(small, ("section", "dp"))
        down_grad, up_grad, pack = [
            jnp.stack(chunks[3 + kind :: -3]).astype(F32) for kind in range(3)
        ]
        qkv_grad, out_grad = pack[:, : 3 * width], pack[:, 3 * width :]
    qkv_grad = qkv_grad.reshape(layers, 3, width, shard).transpose(0, 3, 1, 2)

    gain_rows = small[1:, 0][::-1]
    shift_rows = small[1:, 1][::-1]
    bias_rows = small[:-1, 2][::-1]
    mlp_rows = jnp.stack([small[2 * (layers - 1 - l), 3, :units] for l in range(layers)])
    attn_rows = jnp.stack([small[2 * (layers - 1 - l) + 1, 3:5, :width] for l in range(layers)])

    def own_row(rows_all):
        return lax.dynamic_slice_in_dim(rows_all, section, 1, 0)

    return (
        outputs.reshape(inputs.shape),
        input_grad.reshape(inputs.shape),
        own_row(gain_rows),
        own_row(shift_rows),
        own_row(bias_rows),
        qkv_grad,
        out_grad.transpose(0, 2, 1),
        attn_rows,
        up_grad,
        down_grad,
        mlp_rows,
    )


def solution(mesh):
    placed = (
        P("section", "dp", None, None),
        P(None, "dp", None),
        P("section", "dp", None, None),
        P("section", None),
        P("section", None),
        P("section", None),
        P(None, "dp", None, "tensor"),
        P(None, "dp", "tensor"),
        P(None, None, "tensor"),
        P(None, "dp", "tensor"),
        P(None, "tensor", "dp"),
        P(None, "tensor"),
    )
    return jax.shard_map(
        shards,
        mesh=mesh,
        in_specs=placed,
        out_specs=(
            P("section", "dp", None, None),
            P("section", "dp", None, None),
            P("section", None),
            P("section", None),
            P("section", None),
            P(None, "dp", None, "tensor"),
            P(None, "dp", "tensor"),
            P(None, None, "tensor"),
            P(None, "dp", "tensor"),
            P(None, "tensor", "dp"),
            P(None, "tensor"),
        ),
        check_vma=False,
    )
```

```python
import functools

import jax
import jax.numpy as jnp
from jax import lax
from jax.experimental import pallas as pl
from jax.experimental.pallas import tpu as pltpu
from jax.sharding import PartitionSpec as P

HEAD = 64
EPS = 1e-06
MASKED = -1e30
BF16 = jnp.bfloat16
F32 = jnp.float32
VMEM_LIMIT = 12 * 1024 * 1024
SIDE = ("shuttle", "attn_pack", "mlp_pack")
TINY = ("add", "emit")


def dot_ab(a, b):
    return lax.dot_general(a, b, (((1,), (0,)), ((), ())), preferred_element_type=F32)


def dot_abt(a, b):
    return lax.dot_general(a, b, (((1,), (1,)), ((), ())), preferred_element_type=F32)


def dot_atb(a, b):
    return lax.dot_general(a, b, (((0,), (0,)), ((), ())), preferred_element_type=F32)


SIDE_COST, MAIN_COST, TINY_COST = 1000, 1000, 1000
PASS, ACROSS, EMIT, FORE = 0, 1, 2, 3
MOVES = (
    ((FORE,), (), ()),
    (((PASS, 0),), (), (FORE,)),
    (((ACROSS, 0), (PASS, 1)), (), ((PASS, 2), FORE, (ACROSS, 1), FORE)),
    ((), ((PASS, 3), (ACROSS, 2), (EMIT, 0)), ((ACROSS, 3), (PASS, 4))),
    ((EMIT, 1), (ACROSS, 4), (EMIT, 2), (PASS, 5), (PASS, 6), (ACROSS, 5), (EMIT, 3), (EMIT, 4), (PASS, 7), (EMIT, 5)),
)
PACK, ON, BY = 0, 1, 2
WEIGHTS = (
    ((PACK, 0), (PACK, 1), (ON, 0), (PACK, 2)),
    ((ON, 1), (PACK, 3)),
    (),
    (),
    ((BY, 2), (ON, 2)),
    (),
    ((ON, 3),),
    (),
    ((BY, 3),),
)


def span(start, size):
    return pl.ds(pl.multiple_of(start, size), size)


class Copies:
    def __init__(self, sems):
        self.sems, self.used = sems, 0

    def __call__(self, src, dst):
        copy = pltpu.make_async_copy(src, dst, self.sems.at[self.used])
        self.used += 1
        copy.start()
        return copy

    def all(self, pairs):
        return [self(src, dst) for src, dst in pairs]


def wait(*copies):
    for copy in copies:
        copy.wait()


def normalized(x):
    center = x - jnp.mean(x, axis=-1, keepdims=True)
    rstd = lax.rsqrt(jnp.mean(center * center, axis=-1, keepdims=True) + EPS)
    return center * rstd, rstd


def norm_rows(scal, table, sub_layer):
    return table[jnp.bitwise_xor(scal[3], sub_layer)]


def put_halves(scal, dst, mine, other):
    half = mine.shape[0]
    core = scal[0]
    dst[span(core * half, half), :] = mine[...].astype(F32)
    dst[span((1 - core) * half, half), :] = other[...].astype(F32)


def take_halves(scal, src, mine, other):
    half = mine.shape[0]
    core = scal[0]
    mine[...] = src[span(core * half, half), :].astype(BF16)
    other[...] = src[span((1 - core) * half, half), :].astype(BF16)


def attn_pieces(scal, pieces, dst):
    if len(pieces) == 1:
        return [(pieces[0], dst)]
    own, near, far, direct = pieces
    half, part = own.shape[1], near.shape[0]
    dp, parity = scal[1], scal[2]
    peer = span((1 - dp) * half, half)
    return [
        (own, dst.at[:, span(dp * half, half)]),
        (near, dst.at[span(parity * part, part), peer]),
        (far, dst.at[span((1 - parity) * part, part), peer]),
        (direct, dst.at[pl.ds(2 * part, part), peer]),
    ]


def mlp_pieces(scal, pieces, up, down):
    if len(pieces) == 2:
        return [(pieces[0], up)], [(pieces[1], down)]
    own_up, own_down, near, far, direct = pieces
    half, part = own_up.shape[0], near.shape[0] // 2
    dp, parity = scal[1], scal[2]
    peer = span((1 - dp) * half, half)
    ups = [(own_up, up.at[span(dp * half, half), :])]
    downs = [(own_down, down.at[:, span(dp * half, half)])]
    for piece, index in ((near, parity), (far, 1 - parity), (direct, 2)):
        ups.append(
            (piece.at[pl.ds(0, part), :], up.at[span((1 - dp) * half + index * part, part), :])
        )
        for side in (0, 1):
            downs.append(
                (
                    piece.at[pl.ds(part, part), pl.ds(side * half, half)],
                    down.at[span((2 * index + side) * part, part), peer],
                )
            )
    return ups, downs


def head_mask(width):
    return lax.broadcasted_iota(jnp.int32, (1, width), 1) // HEAD


def only(mask, values):
    return jnp.where(mask, values, jnp.zeros((), values.dtype))


def attn_pack(layer, scal, qkv, out, own, shared, direct, wide, low, sems):
    copy = Copies(sems)
    part = shared.shape[0]
    count = qkv.shape[1]
    rest = count - 2 * part
    loads = []
    for index in (scal[2], 1 - scal[2]):
        here = span(index * part, part)
        loads.append((here, [copy(qkv.at[layer, here], wide.at[here])]))
    loads.append(
        (
            pl.ds(2 * part, part),
            [
                copy(qkv.at[layer, pl.ds(2 * part, rest)], wide.at[pl.ds(2 * part, rest)]),
                copy(out.at[layer], wide.at[pl.ds(count, part - rest)]),
            ],
        )
    )
    keep = []
    for (here, copies), piece in zip(loads, (shared, None, direct)):
        wait(*copies)
        third = wide[here, :].astype(BF16)
        low[here, :] = third
        if piece is not None:
            piece[...] = third
        keep.append(copy(low.at[here], own.at[here]))
    wait(*keep)


def mlp_pack(
    layer, scal, up, down, own_up, own_down, shared, direct, wide_up, wide_down, low_up, low_down,
    sems,
):
    copy = Copies(sems)
    half, part = wide_up.shape[0], shared.shape[0] // 2
    loads = []
    for index in (scal[2], 1 - scal[2], 2):
        here, there = span(index * part, part), span(2 * index * part, 2 * part)
        loads.append(
            (
                here,
                there,
                copy(up.at[layer, here], wide_up.at[here]),
                copy(down.at[layer, there], wide_down.at[there]),
            )
        )
    keep = []
    for (here, there, *copies), piece in zip(loads, (shared, None, direct)):
        wait(*copies)
        third_up, third_down = wide_up[here, :].astype(BF16), wide_down[there, :].astype(BF16)
        low_up[here, :] = third_up
        low_down[there, :] = third_down
        keep.append(copy(low_up.at[here], own_up.at[here]))
        keep.append(copy(low_down.at[there], own_down.at[there]))
        if piece is not None:
            piece[:part, :] = third_up
            piece[part:, :half] = third_down[:part]
            piece[part:, half:] = third_down[part:]
    wait(*keep)


def residual(scal, table, sub_layer, refs, x_out):
    x_prev, mine, other = refs
    put_halves(scal, x_out, mine, other)
    bias = norm_rows(scal, table, sub_layer - 1)[2:3]
    x_out[...] = x_prev[...] + (x_out[...] + bias)
    return x_out[...]


def attn_forward(sub_layer, scal, table, *refs):
    if sub_layer == 0:
        x_ref, refs = refs[0], refs[1:]
    else:
        res, refs = refs[:3], refs[3:]
    (seg_col, seg_row, inner, w), refs = refs[:4], refs[4:]
    if sub_layer:
        x_ref, refs = refs[0], refs[1:]
        residual(scal, table, sub_layer, res, x_ref)
    low_out, qkv_out, soft_out, ctx_out, mine, other, total = refs
    x = x_ref[...]
    xhat, _ = normalized(x)
    norm = norm_rows(scal, table, sub_layer)
    low = (xhat * norm[0:1] + norm[1:2]).astype(BF16)
    low_out[...] = low
    width = ctx_out.shape[1]
    q = (dot_abt(low, w[:width]) + inner[0:1, :]).astype(BF16)
    k = dot_abt(low, w[width : 2 * width]).astype(BF16)
    v = (dot_abt(low, w[2 * width : 3 * width]) + inner[1:2, :]).astype(BF16)
    qkv_out[0] = q
    qkv_out[1] = k
    qkv_out[2] = v
    same = seg_col[...] == seg_row[...]
    heads = head_mask(width)
    context = jnp.zeros((x.shape[0], width), F32)
    for h in range(width // HEAD):
        scores = dot_abt(only(heads == h, q), k) * HEAD ** (-0.5)
        scores = jnp.where(same, scores, MASKED)
        expanded = jnp.exp(scores - jnp.max(scores, axis=-1, keepdims=True))
        soft = expanded / jnp.sum(expanded, axis=-1, keepdims=True)
        soft_out[h] = soft
        context = context + dot_ab(soft.astype(BF16), only(heads == h, v))
    context = context.astype(BF16)
    ctx_out[...] = context
    total[...] = dot_ab(context, w[3 * width :])
    take_halves(scal, total, mine, other)


def mlp_forward(sub_layer, count, scal, table, *refs):
    res, up_bias, up, down, refs = refs[:3], refs[3], refs[4], refs[5], refs[6:]
    if count:
        cotangent, refs = refs[0], refs[1:]
        x_out, mine, other, small, back_mine, back_other = refs[:6]
        grads, (total, full) = refs[6:-2], refs[-2:]
    else:
        x_out, low_out, active_out, slope_out, mine, other, total = refs
    x = residual(scal, table, sub_layer, res, x_out)
    xhat, _ = normalized(x)
    norm = norm_rows(scal, table, sub_layer)
    low = (xhat * norm[0:1] + norm[1:2]).astype(BF16)
    hidden = dot_ab(low, up[...]) + up_bias[...]
    phi = 0.5 * (1.0 + lax.erf(hidden * 0.7071067811865476))
    slope = phi + hidden * (0.3989422804014327 * jnp.exp(-0.5 * hidden * hidden))
    active = (hidden * phi).astype(BF16)
    if count:
        small[...] = jnp.zeros_like(small)
        mlp_back_part(
            scal, count, cotangent[...], low, active, up, down, slope, small, back_mine, back_other,
            grads, total, full,
        )
    else:
        low_out[...] = low
        active_out[...] = active
        slope_out[...] = slope
    total[...] = dot_ab(active, down[...])
    take_halves(scal, total, mine, other)


def norm_backward(scal, table, sub_layer, g_prev, mine, other, x, g_out, small):
    put_halves(scal, g_out, mine, other)
    d_normed = g_out[...]
    xhat, rstd = normalized(x[...])
    small[0:1, :] = jnp.sum(d_normed * xhat, axis=0, keepdims=True)
    small[1:2, :] = jnp.sum(d_normed, axis=0, keepdims=True)
    d_hat = d_normed * norm_rows(scal, table, sub_layer)[0:1]
    inner = jnp.mean(d_hat * xhat, axis=-1, keepdims=True)
    g = g_prev[...] + (d_hat - jnp.mean(d_hat, axis=-1, keepdims=True) - xhat * inner) * rstd
    g_out[...] = g
    return g


def mlp_back_part(
    scal, count, g, low, active, up, down, slope, small, mine, other, grads, total, full
):
    small[2:3, :] = jnp.sum(g, axis=0, keepdims=True)
    g_low = g.astype(BF16)
    full[...] = dot_atb(active, g_low)
    column_halves(scal, full, grads[: len(grads) // 2])
    d_hidden = (dot_abt(g_low, down[...]) * slope).astype(BF16)
    small[3:4, :] = jnp.sum(d_hidden.astype(F32), axis=0, keepdims=True)
    total[...] = dot_abt(d_hidden, up[...])
    take_halves(scal, total, mine, other)
    full[...] = dot_atb(low, d_hidden)
    row_halves(scal, full, grads[len(grads) // 2 :])


def mlp_backward(sub_layer, scal, table, *refs):
    res, (low, active, slope, up, down), refs = refs[:4], refs[4:9], refs[9:]
    g_out, small, mine, other = refs[:4]
    grads, (total, full) = refs[4:-2], refs[-2:]
    small[...] = jnp.zeros_like(small)
    g = norm_backward(scal, table, sub_layer + 1, *res, g_out, small)
    mlp_back_part(
        scal, 0, g, low[...], active[...], up, down, slope[...], small, mine, other, grads, total,
        full,
    )


def attn_backward(sub_layer, scal, table, *refs):
    res, (low, qkv, soft_all, ctx, w), refs = refs[:4], refs[4:9], refs[9:]
    g_out, small, mine, other = refs[:4]
    grads, (total, full) = refs[4:-2], refs[-2:]
    small[...] = jnp.zeros_like(small)
    g = norm_backward(scal, table, sub_layer + 1, *res, g_out, small)
    small[2:3, :] = jnp.sum(g, axis=0, keepdims=True)
    g_low = g.astype(BF16)
    q, k, v = qkv[0], qkv[1], qkv[2]
    width = q.shape[1]
    heads = head_mask(width)
    d_context = dot_abt(g_low, w[3 * width :]).astype(BF16)
    d_q = jnp.zeros(q.shape, F32)
    d_k = jnp.zeros(q.shape, F32)
    d_v = jnp.zeros(q.shape, F32)
    for h in range(width // HEAD):
        soft = soft_all[h]
        d_here = only(heads == h, d_context)
        d_soft = dot_abt(d_here, v)
        d_v = d_v + dot_atb(soft.astype(BF16), d_here)
        weighted = soft * d_soft
        delta = jnp.sum(weighted, axis=-1, keepdims=True)
        d_scores = (weighted - soft * delta).astype(BF16)
        d_q = d_q + dot_ab(d_scores, only(heads == h, k))
        d_k = d_k + dot_atb(d_scores, only(heads == h, q))
    d_q = (d_q * HEAD ** (-0.5)).astype(BF16)
    d_k = (d_k * HEAD ** (-0.5)).astype(BF16)
    d_v = d_v.astype(BF16)
    small[3:4, :width] = jnp.sum(d_q.astype(F32), axis=0, keepdims=True)
    small[4:5, :width] = jnp.sum(d_v.astype(F32), axis=0, keepdims=True)
    total[...] = (
        dot_ab(d_q, w[:width])
        + dot_ab(d_k, w[width : 2 * width])
        + dot_ab(d_v, w[2 * width : 3 * width])
    )
    take_halves(scal, total, mine, other)
    for index, part in enumerate((d_q, d_k, d_v)):
        full[index * width : (index + 1) * width, :] = dot_atb(part, low[...])
    full[3 * width :, :] = dot_atb(ctx[...], g_low)
    column_halves(scal, full, grads)


def output(last, scal, table, x_last, mine, other, out_hbm, token, out, sems):
    token[...] = jnp.zeros_like(token)
    residual(scal, table, last, (x_last, mine, other), out)
    wait(Copies(sems)(out, out_hbm))


def input_backward(scal, table, *refs):
    res, refs = refs[:4], refs[4:]
    g_hbm, small, g_out, sems = refs
    small[...] = jnp.zeros_like(small)
    norm_backward(scal, table, 0, *res, g_out, small)
    wait(Copies(sems)(g_out, g_hbm))


SMALL_ROWS = 16


def input_backward_packed(scal, table, *refs):
    res, smalls, parts, refs = refs[:4], refs[4:8], refs[8:10], refs[10:]
    g_hbm, *outs, g_out, small, packed, sems = refs
    norm_backward(scal, table, 0, *res, g_out, small)
    keep = Copies(sems)(g_out, g_hbm)
    packed[...] = jnp.zeros_like(packed)
    layers = len(smalls) // 2
    count = 2 * layers
    norms = [small, *smalls]
    for s in range(count):
        packed[s : s + 1, :] = norms[s][0:1, :]
        packed[count + s : count + s + 1, :] = norms[s][1:2, :]
        packed[2 * count + s : 2 * count + s + 1, :] = smalls[s][2:3, :]
    row = 3 * count
    width = packed.shape[1] // (2 * layers)
    for layer in range(layers):
        packed[row + layer : row + layer + 1, :] = smalls[2 * layer + 1][3:4, :]
        for part in range(2):
            lane = (2 * layer + part) * width
            packed[row + layers : row + layers + 1, lane : lane + width] = smalls[2 * layer][
                3 + part : 4 + part, :width
            ]
    for part, out in zip(parts, outs):
        rows, half = part.shape
        out[:rows, :] = part[...]
        out[rows : rows + SMALL_ROWS, :] = packed[:, :half].astype(BF16)
        out[rows + SMALL_ROWS :, :] = packed[:, half:].astype(BF16)
    wait(keep)


def column_halves(scal, full, outs):
    if len(outs) == 1:
        outs[0][...] = full[...].astype(BF16)
        return
    count = len(outs) // 2
    rows, half = outs[0].shape
    for index in range(count):
        own, peer = outs[2 * index], outs[2 * index + 1]
        here = slice(index * rows, (index + 1) * rows)
        own[...] = full[here, span(scal[1] * half, half)].astype(BF16)
        peer[...] = full[here, span((1 - scal[1]) * half, half)].astype(BF16)


def row_halves(scal, full, outs):
    if len(outs) == 1:
        outs[0][...] = full[...].astype(BF16)
        return
    half = outs[0].shape[1]
    for out, index in zip(outs, (scal[1], 1 - scal[1])):
        for side in (0, 1):
            out[side * half : (side + 1) * half, :] = full[
                span(index * half, half), side * half : (side + 1) * half
            ].astype(BF16)


def inner_section(scal):
    return (scal[3] == 1) | (scal[3] == 2)


def pass_kernel(mine, totals, scal, *refs):
    *refs, out = refs
    if not totals:
        out[...] = refs[0][...] + refs[1][...]
        return
    if not mine:
        out[...] = refs[-2][...] + refs[-1][...]
        return

    @pl.when(inner_section(scal))
    def _():
        rows = refs[2].shape[0]
        out[:rows, :] = refs[2][...] + refs[3][...]
        if rows < out.shape[0]:
            out[rows:, :] = jnp.zeros((out.shape[0] - rows, out.shape[1]), out.dtype)

    @pl.when(jnp.logical_not(inner_section(scal)))
    def _():
        rows = refs[0].shape[0]
        out[:rows, :] = refs[0][...] + refs[1][...]
        if rows < out.shape[0]:
            out[rows:, :] = jnp.zeros((out.shape[0] - rows, out.shape[1]), out.dtype)


def near_kernel(own, peer, arrived, out):
    out[...] = (own[...] + peer[...]) + arrived[: out.shape[0], :]


def emit_sums(kind, layer, small, aliased, scal, held, sent, *refs):
    refs = refs[aliased:]
    *outs, token, wide, sems = refs
    token[...] = jnp.zeros_like(token)
    rows, half = wide.shape

    def put(block):
        if kind == "up":
            for side in (0, 1):
                wide[:, side * rows : (side + 1) * rows] = block[
                    side * rows : (side + 1) * rows, :
                ].astype(F32)
        else:
            wide[...] = block[:rows, :].astype(F32)

    @pl.when(inner_section(scal))
    def _():
        put(held)

    @pl.when(jnp.logical_not(inner_section(scal)))
    def _():
        put(sent)

    copy = Copies(sems)
    copies, row = [], 0
    for out in outs[: len(outs) - small]:
        copies.append(copy(wide.at[pl.ds(row, out.shape[1])], out.at[layer]))
        row += out.shape[1]
    if small:
        *norms, mlp_bias, attn_bias = outs[-small:]
        layers, count = mlp_bias.shape[0], 2 * mlp_bias.shape[0]
        for index, norm in enumerate(norms):
            here = row + index * count + scal[3]
            norm[:, :half] = wide[pl.ds(here, 1), :]
            norm[:, half:] = wide[pl.ds(here + SMALL_ROWS, 1), :]
        here = row + 3 * count
        mlp_bias[:, :half] = wide[here : here + layers, :]
        mlp_bias[:, half:] = wide[here + SMALL_ROWS : here + SMALL_ROWS + layers, :]
        here += layers
        width = attn_bias.shape[1]
        for index in range(attn_bias.shape[0]):
            line = here + SMALL_ROWS * (index * width // half)
            lane = index * width % half
            attn_bias[index : index + 1, :] = wide[line : line + 1, lane : lane + width]
    wait(*copies)


def shuttle(plan, count, scal, *refs):
    refs, sems = refs[:-1], refs[-1]
    copy = Copies(sems)
    wait(*[copy(src, dst) for src, dst in plan(scal, refs[:count], refs[count:])])


SPACES = {"H": pltpu.HBM, "V": pltpu.VMEM, "W": pltpu.VMEM, "S": pltpu.SMEM, "A": pl.ANY}


def call(body, name, operands, outs, scratch=(), copies=0, aliases=None):
    def shape_of(shape, dtype, place):
        return jax.ShapeDtypeStruct(shape, dtype) if place == "W" else SPACES[place](shape, dtype)

    sems = [pltpu.SemaphoreType.DMA((copies,))] if copies else []
    return pl.pallas_call(
        body,
        out_shape=[shape_of(*out) for out in outs],
        in_specs=[pl.BlockSpec(memory_space=SPACES[place]) for _, place in operands],
        out_specs=[pl.BlockSpec(memory_space=SPACES[place]) for _, _, place in outs],
        scratch_shapes=[pltpu.VMEM(s, d) for s, d in scratch] + sems,
        input_output_aliases=aliases or {},
        compiler_params=pltpu.CompilerParams(vmem_limit_bytes=VMEM_LIMIT),
        cost_estimate=pl.CostEstimate(
            flops=SIDE_COST if name in SIDE else TINY_COST if name in TINY else MAIN_COST,
            bytes_accessed=1000,
            transcendentals=0,
        ),
        name=name,
    )(
        *[
            pltpu.with_memory_space_constraint(array, pltpu.HBM) if place == "H" else array
            for array, place in operands
        ]
    )


def pairs_xor(axis, bit):
    return [(i, i ^ bit) for i in range(lax.axis_size(axis))]


class Order:
    def __init__(self):
        self.tokens = []

    def hold(self, *arrays):
        held = lax.optimization_barrier(tuple(arrays) + tuple(self.tokens))
        self.tokens = list(held)
        return held[: len(arrays)]

    def run(self, body, name, operands, *args, **kwargs):
        tokens, count = self.tokens, len(operands)

        def kernel(*refs):
            body(*refs[:count], *refs[count + len(tokens) :])

        operands = list(operands) + [(token, "A") for token in tokens]
        out = call(kernel, name, operands, *args, **kwargs)
        self.tokens = [out[-1]]
        return out


def add_kernel(held, sent, out):
    out[...] = held[...] + sent[...]


def add(order, held, sent):
    [out] = order.run(
        add_kernel, "add", [(held, "W"), (sent, "W")], [(held.shape, held.dtype, "W")]
    )
    return out


class Pipeline:
    def __init__(self, order, scal, count):
        self.order, self.scal, self.count = order, scal, count
        self.own, self.peer = [], []
        self.passed, self.outer, self.near, self.middle = {}, {}, {}, {}

    def put(self, own, peer):
        self.own.append(own)
        self.peer.append(lax.ppermute(peer, "dp", pairs_xor("dp", 1)))

    def run(self, kernel, name, arrays, shape, scal=()):
        operands = [*scal, *[(array, "W") for array in arrays]]
        return self.order.run(kernel, name, operands, [(shape, BF16, "W")])[0]

    def pass_on(self, t):
        mine = [self.own[t], self.peer[t]] if t < self.count else []
        totals = [self.near[t - 2], self.middle[t - 2]] if t >= 2 else []
        arrays = mine + totals
        shape = max(array.shape for array in arrays)
        kernel = functools.partial(pass_kernel, bool(mine), bool(totals))
        self.passed[t] = self.run(kernel, "add", arrays, shape, [self.scal])
        pairs = ([(0, 1), (3, 2)] if mine else []) + ([(1, 0), (2, 3)] if totals else [])
        self.outer[t] = lax.ppermute(self.passed[t], "section", pairs)

    def across(self, t):
        arrays = [self.own[t], self.peer[t], self.outer[t]]
        self.near[t] = self.run(near_kernel, "add", arrays, self.own[t].shape)
        self.middle[t] = lax.ppermute(self.near[t], "section", [(1, 2), (2, 1)])

    def total(self, t):
        return self.passed[t + 2], self.outer[t + 2], self.own[t].shape[0]


def shards(
    inputs,
    segments,
    cotangent,
    norm_gain,
    norm_shift,
    out_bias,
    attn_qkv,
    attn_out,
    attn_bias,
    mlp_in,
    mlp_out,
    mlp_bias,
):
    section = lax.axis_index("section")
    dp = lax.axis_index("dp")
    tensor = lax.axis_index("tensor")
    dp_count = lax.axis_size("dp")
    layers = attn_qkv.shape[0]
    rows, model = inputs.shape[2], inputs.shape[3]
    half = rows // 2
    shard = attn_qkv.shape[1]
    width = attn_out.shape[2]
    units = mlp_in.shape[2]
    heads = width // HEAD
    core = tensor % 2
    scal = (jnp.stack([core, dp, section % 2, section]).astype(jnp.int32), "S")
    paired = dp_count == 2
    order = Order()

    def places(place, arrays):
        return [(array, place) for array in arrays]

    table = jnp.concatenate([norm_gain, norm_shift, out_bias], axis=0)
    table = jnp.pad(table, ((0, 5), (0, 0)))[None]
    for bit in (1, 2):
        table = jnp.concatenate([table, lax.ppermute(table, "section", pairs_xor("section", bit))])
    table = (table, "V")

    qkv_t = attn_qkv.transpose(0, 2, 3, 1).reshape(layers, 3 * width, shard)
    out_t = attn_out.transpose(0, 2, 1)

    def sent(shared, direct):
        near = lax.ppermute(shared, "dp", pairs_xor("dp", 1))
        return [near, None, lax.ppermute(direct, "dp", pairs_xor("dp", 1))]

    def send_on(weights):
        if paired:
            [weights[-3]] = order.hold(weights[-3])
            weights[-2] = lax.ppermute(weights[-3], "section", pairs_xor("section", 1))

    def arrived(weights):
        if paired:
            [weights[-1]] = order.hold(weights[-1])

    def attn_gather(layer):
        if not paired:
            pack = jnp.concatenate([qkv_t[layer], out_t[layer]], axis=0).astype(BF16)
            return [lax.all_gather(pack, "dp", axis=1, tiled=True)]
        third = 4 * width // 3
        own, shared, direct = order.run(
            functools.partial(attn_pack, layer),
            "attn_pack",
            [scal, (qkv_t, "H"), (out_t, "H")],
            [((4 * width, shard), BF16, "H")] + [((third, shard), BF16, "V")] * 2,
            [((4 * width, shard), F32), ((4 * width, shard), BF16)],
            copies=7,
        )
        return [own, *sent(shared, direct)]

    def mlp_gather(layer):
        if not paired:
            return [
                lax.all_gather(mlp_in[layer].astype(BF16), "dp", axis=0, tiled=True),
                lax.all_gather(mlp_out[layer].astype(BF16), "dp", axis=1, tiled=True),
            ]
        third = 2 * shard // 3
        own_up, own_down, shared, direct = order.run(
            functools.partial(mlp_pack, layer),
            "mlp_pack",
            [scal, (mlp_in, "H"), (mlp_out, "H")],
            [((shard, units), BF16, "H"), ((units, shard), BF16, "H")]
            + [((third, units), BF16, "V")] * 2,
            [(shape, kind) for kind in (F32, BF16) for shape in ((shard, units), (units, shard))],
            copies=12,
        )
        return [own_up, own_down, *sent(shared, direct)]

    seg = lax.dynamic_index_in_dim(segments[:, 0], section, 0, keepdims=False)
    segs = [(seg[:, None], "V"), (seg[None, :], "V")]

    row_f32, row_low = ((rows, model), F32), ((rows, model), BF16)
    unit_f32, unit_low = ((rows, units), F32), ((rows, units), BF16)
    half_low = ((half, model), BF16)
    small_out = ((8, model), F32, "W")
    qkv_low, soft_f32 = ((3, rows, width), BF16), ((heads, rows, rows), F32)
    ctx_low, attn_full = ((rows, width), BF16), ((4 * width, model), BF16)
    up_full, down_full = ((model, units), BF16), ((units, model), BF16)

    def held(*shapes):
        return [shape + ("V",) for shape in shapes]

    def move_data(save=(), fetch=(), attn=None, mlp=None):
        pieces = attn or mlp or []

        def plan(scal, ins, outs):
            count = len(save) + len(fetch)
            pairs = list(zip(ins[:count], outs[:count]))
            if attn:
                pairs += attn_pieces(scal, ins[count:], outs[count])
            if mlp:
                ups, downs = mlp_pieces(scal, ins[count:], *outs[count:])
                pairs += ups + downs
            return pairs

        outs = [(array.shape, array.dtype, "H") for array in save]
        outs += [(array.shape, array.dtype, "V") for array in fetch]
        outs += held(attn_full) if attn else held(up_full, down_full) if mlp else []
        operands = places("V", save) + places("H", list(fetch) + list(pieces))
        return order.run(
            functools.partial(shuttle, plan, len(operands)),
            "shuttle",
            [scal, *operands],
            outs,
            copies=len(save) + len(fetch) + (11 if mlp else 4),
        )

    def nothing():
        return None

    def tensor_sum(mine, other, window=nothing, ahead=nothing, moves=((), (), ())):
        arrived = lax.ppermute(other, "tensor", pairs_xor("tensor", 1))
        ahead()
        move(*moves[0])
        near = add(order, mine, arrived)
        arrived = lax.ppermute(near, "tensor", pairs_xor("tensor", 2))
        window()
        move(*moves[1])
        total = add(order, near, arrived)
        arrived = lax.ppermute(total, "tensor", pairs_xor("tensor", 1))
        move(*moves[2])
        return [total, arrived]

    def fore_steps(mine, other):
        arrived = lax.ppermute(other, "tensor", pairs_xor("tensor", 1))
        yield
        near = add(order, mine, arrived)
        arrived = lax.ppermute(near, "tensor", pairs_xor("tensor", 2))
        yield
        total = add(order, near, arrived)
        arrived = lax.ppermute(total, "tensor", pairs_xor("tensor", 1))
        yield
        out, _ = order.run(
            functools.partial(output, 2 * layers),
            "output",
            [scal, table, *places("V", [x3, total, arrived])],
            [row_f32 + ("H",), ((8, 128), F32, "V")],
            [row_f32],
            copies=1,
        )
        yield out

    def attn_step(s, res, w):
        return order.run(
            functools.partial(attn_forward, s),
            "attn_forward",
            [scal, table, *places("V", res), *segs, *places("V", [attn_bias[s // 2], w])],
            held(*([row_f32] if s else []), row_low, qkv_low, soft_f32, ctx_low, half_low, half_low),
            [row_f32],
        )

    def mlp_step(s, res, up, down, cotangent=None):
        last = cotangent is not None
        operands = [*res, mlp_bias[s // 2][None], up, down] + ([cotangent] if last else [])
        if last:
            grads = mlp_shapes()
            outs = held(row_f32, half_low, half_low) + [small_out] + held(half_low, half_low)
            outs += grads
        else:
            grads = []
            outs = held(row_f32, row_low, unit_low, unit_f32, half_low, half_low)
        return order.run(
            functools.partial(mlp_forward, s, len(grads)),
            "mlp_forward",
            [scal, table, *places("V", operands)],
            outs,
            [row_f32] + ([(up_full[0], F32)] if last else []),
        )

    def mlp_shapes():
        if not paired:
            return [(down_full[0], BF16, "W"), (up_full[0], BF16, "W")]
        return [((units, shard), BF16, "W")] * 4

    def attn_shapes():
        if not paired:
            return [(attn_full[0], BF16, "W")]
        return [((4 * width, shard), BF16, "W")] * 2

    chunks = []
    pipeline = Pipeline(order, scal, 3 * layers)

    def add_chunks(parts, axis):
        if not paired:
            whole = lax.psum_scatter(parts[0], "dp", scatter_dimension=axis, tiled=True)
            chunks.append(lax.psum(whole, "section"))
            return
        for own, peer in zip(parts[0::2], parts[1::2]):
            pipeline.put(own, peer)

    emitted = {}

    def emit(kind, layer, index):
        shape = {"up": (shard, units), "down": (units, shard), "attn": (4 * width, shard)}[kind]
        token = ((8, 128), F32, "V")
        outs = [((layers,) + shape, F32, "H")]
        if kind == "attn":
            outs = [((layers, count, shard), F32, "H") for count in (3 * width, width)]
        before = emitted.get(kind, [])
        held_sum, sent_sum, rows_all = pipeline.total(index)
        operands = [held_sum, sent_sum]
        wide = shape if kind == "up" else (rows_all, shape[1])
        smalls = []
        if kind == "attn" and rows_all > shape[0]:
            smalls = [((1, model), F32, "W")] * 3
            smalls += [((layers, units), F32, "W"), ((2 * layers, width), F32, "W")]
        *emitted[kind], _ = order.run(
            functools.partial(emit_sums, kind, layer, len(smalls), len(before)),
            "emit",
            [scal, *places("W", operands), *places("H", before)],
            [*outs, *smalls, token],
            [(wide, F32)],
            copies=2,
            aliases={1 + len(operands) + index: index for index in range(len(before))},
        )

    def move(*indices):
        for index in indices:
            if index == FORE:
                fore.append(next(fore[0]))
            elif not paired:
                continue
            else:
                step, t = index
                if step == EMIT:
                    emit(("down", "up", "attn")[t % 3], layers - 1 - t // 3, t)
                else:
                    (pipeline.pass_on if step == PASS else pipeline.across)(t)

    def mlp_chunks(parts):
        add_chunks(parts[: len(parts) // 2], 1)
        add_chunks(parts[len(parts) // 2 :], 0)

    def back(body, name, s, operands, full, grads):
        return order.run(
            functools.partial(body, s),
            name,
            [scal, table, *places("V", operands)],
            held(row_f32) + [small_out] + held(half_low, half_low) + grads,
            [row_f32, (full[0], F32)],
        )

    box = {}

    def keep(names, values):
        box.update(zip(names, values))

    def kept(*names):
        return [box[name] for name in names]

    x0 = inputs.reshape(rows, model)
    pieces = {}

    def weigh(*steps):
        for step, s in steps:
            if step == PACK:
                pieces[s] = (mlp_gather if s % 2 else attn_gather)(s // 2)
            else:
                (send_on if step == ON else arrived)(pieces[s])

    weigh(*WEIGHTS[0])
    [w] = move_data(attn=pieces[0])
    low, qkv, soft, ctx, *halves = attn_step(0, [x0], w)

    def window():
        weigh(*WEIGHTS[2])
        keep(
            ("low0", "qkv0", "soft0", "ctx0", "up", "down"),
            move_data([low, qkv, soft, ctx], mlp=pieces[1]),
        )
        weigh(*WEIGHTS[3])

    total = tensor_sum(*halves, window, lambda: weigh(*WEIGHTS[1]))
    x1, low, active, slope, *halves = mlp_step(1, [x0, *total], box["up"], box["down"])

    def window():
        weigh(*WEIGHTS[5])
        keep(
            ("x1", "low1", "active1", "slope1", "w"),
            move_data([x1, low, active, slope], attn=pieces[2]),
        )
        weigh(*WEIGHTS[6])

    total = tensor_sum(*halves, window, lambda: weigh(*WEIGHTS[4]))
    x2, low, qkv, soft, ctx, *halves = attn_step(2, [x1, *total], box["w"])

    def window():
        weigh(*WEIGHTS[8])
        keep(
            ("x2", "low2", "qkv2", "soft2", "ctx2", "up", "down"),
            move_data([x2, low, qkv, soft, ctx], mlp=pieces[3]),
        )

    total = tensor_sum(*halves, window, lambda: weigh(*WEIGHTS[7]))
    g = cotangent.reshape(rows, model)
    x3, fore_mine, fore_other, small3, *rest = mlp_step(
        3, [x2, *total], box["up"], box["down"], g
    )
    fore = [fore_steps(fore_mine, fore_other)]

    def window():
        keep(
            ("low", "ctx", "qkv", "soft", "w"),
            move_data(fetch=kept("low2", "ctx2", "qkv2", "soft2"), attn=pieces[2]),
        )

    total = tensor_sum(*rest[:2], window, lambda: mlp_chunks(rest[2:]), MOVES[0])
    operands = [g, *total, x3, *kept("low", "qkv", "soft", "ctx", "w")]
    g, small2, *rest = back(
        attn_backward, "attn_backward", 2, operands, attn_full, attn_shapes()
    )

    def window():
        keep(
            ("x", "low", "active", "slope", "up", "down"),
            move_data(fetch=kept("x2", "low1", "active1", "slope1"), mlp=pieces[1]),
        )

    total = tensor_sum(*rest[:2], window, lambda: add_chunks(rest[2:], 1), MOVES[1])
    operands = [g, *total, *kept("x", "low", "active", "slope", "up", "down")]
    g, small1, *rest = back(mlp_backward, "mlp_backward", 1, operands, up_full, mlp_shapes())

    def window():
        keep(
            ("x", "low", "ctx", "qkv", "soft", "w"),
            move_data(fetch=kept("x1", "low0", "ctx0", "qkv0", "soft0"), attn=pieces[0]),
        )

    total = tensor_sum(*rest[:2], window, lambda: mlp_chunks(rest[2:]), MOVES[2])
    operands = [g, *total, *kept("x", "low", "qkv", "soft", "ctx", "w")]
    g, small0, *rest = back(
        attn_backward, "attn_backward", 0, operands, attn_full, attn_shapes()
    )
    last_parts = rest[2:]

    def grads():
        if not paired:
            add_chunks(last_parts, 1)

    total = tensor_sum(*rest[:2], ahead=grads, moves=MOVES[3])
    operands = [g, *total, x0]
    if paired:
        rows_all = 4 * width + 2 * SMALL_ROWS
        input_grad, own, peer = order.run(
            input_backward_packed,
            "input_backward",
            [scal, table, *places("V", [*operands, small0, small1, small2, small3, *last_parts])],
            [row_f32 + ("H",)] + [((rows_all, shard), BF16, "W")] * 2,
            [row_f32, ((8, model), F32), ((SMALL_ROWS, model), F32)],
            copies=1,
        )
        add_chunks([own, peer], 1)
        move(*MOVES[4])
        [up_grad], [down_grad], (qkv_grad, out_grad, *smalls) = (
            emitted[kind] for kind in ("up", "down", "attn")
        )
        gain_grad, shift_grad, bias_grad, mlp_rows, attn_rows = smalls
        attn_rows = attn_rows.reshape(layers, 2, width)
    else:
        input_grad, small = order.run(
            input_backward,
            "input_backward",
            [scal, table, *places("V", operands)],
            [row_f32 + ("H",), small_out],
            [row_f32],
            copies=1,
        )
        small = jnp.stack([small, small0, small1, small2, small3])
        small = lax.psum(small, ("section", "dp"))
        down_grad, up_grad, pack = [
            jnp.stack(chunks[3 + kind :: -3]).astype(F32) for kind in range(3)
        ]
        qkv_grad, out_grad = pack[:, : 3 * width], pack[:, 3 * width :]
        gain_grad, shift_grad, bias_grad = [
            lax.dynamic_slice_in_dim(rows_all, section, 1, 0)
            for rows_all in (small[:-1, 0], small[:-1, 1], small[1:, 2])
        ]
        mlp_rows = jnp.stack([small[2 * layer + 2, 3, :units] for layer in range(layers)])
        attn_rows = jnp.stack([small[2 * layer + 1, 3:5, :width] for layer in range(layers)])
    while len(fore) < 5:
        move(FORE)
    outputs = fore[4]
    qkv_grad = qkv_grad.reshape(layers, 3, width, shard).transpose(0, 3, 1, 2)

    return (
        outputs.reshape(inputs.shape),
        input_grad.reshape(inputs.shape),
        gain_grad,
        shift_grad,
        bias_grad,
        qkv_grad,
        out_grad.transpose(0, 2, 1),
        attn_rows,
        up_grad,
        down_grad,
        mlp_rows,
    )


def solution(mesh):
    placed = (
        P("section", "dp", None, None),
        P(None, "dp", None),
        P("section", "dp", None, None),
        P("section", None),
        P("section", None),
        P("section", None),
        P(None, "dp", None, "tensor"),
        P(None, "dp", "tensor"),
        P(None, None, "tensor"),
        P(None, "dp", "tensor"),
        P(None, "tensor", "dp"),
        P(None, "tensor"),
    )
    return jax.shard_map(
        shards,
        mesh=mesh,
        in_specs=placed,
        out_specs=(
            P("section", "dp", None, None),
            P("section", "dp", None, None),
            P("section", None),
            P("section", None),
            P("section", None),
            P(None, "dp", None, "tensor"),
            P(None, "dp", "tensor"),
            P(None, None, "tensor"),
            P(None, "dp", "tensor"),
            P(None, "tensor", "dp"),
            P(None, "tensor"),
        ),
        check_vma=False,
    )
```

```python
import functools

import jax
import jax.numpy as jnp
from jax import lax
from jax.experimental import pallas as pl
from jax.experimental.pallas import tpu as pltpu
from jax.sharding import PartitionSpec as P

HEAD = 64
EPS = 1e-06
MASKED = -1e30
BF16 = jnp.bfloat16
F32 = jnp.float32
VMEM_LIMIT = 12 * 1024 * 1024
SIDE = ("shuttle", "attn_pack", "mlp_pack")
TINY = ("add", "emit")


def dot_ab(a, b):
    return lax.dot_general(a, b, (((1,), (0,)), ((), ())), preferred_element_type=F32)


def dot_abt(a, b):
    return lax.dot_general(a, b, (((1,), (1,)), ((), ())), preferred_element_type=F32)


def dot_atb(a, b):
    return lax.dot_general(a, b, (((0,), (0,)), ((), ())), preferred_element_type=F32)


SIDE_COST, MAIN_COST, TINY_COST = 1000, 1000, 1000
PASS, ACROSS, EMIT, FORE, SMALL = 0, 1, 2, 3, 4
MOVES = (
    ((FORE,), (), ()),
    (((PASS, 0),), (FORE,), ()),
    (((ACROSS, 0), (PASS, 1), FORE), ((PASS, 2),), ((ACROSS, 1), FORE)),
    (((PASS, 3),), ((ACROSS, 2), (EMIT, 0)), ((PASS, 4), (ACROSS, 3), (EMIT, 1))),
    (SMALL, (PASS, 5), (ACROSS, 4), (EMIT, 2), SMALL, (PASS, 6), (ACROSS, 5), (EMIT, 3), SMALL, (EMIT, 4), (PASS, 7), SMALL, (EMIT, 5)),
)
PACK, ON, BY = 0, 1, 2
WEIGHTS = (
    ((PACK, 0), (PACK, 1), (ON, 0), (PACK, 2)),
    ((ON, 1), (PACK, 3)),
    (),
    (),
    ((BY, 2), (ON, 2)),
    (),
    ((ON, 3),),
    (),
    ((BY, 3),),
)


def span(start, size):
    return pl.ds(pl.multiple_of(start, size), size)


class Copies:
    def __init__(self, sems):
        self.sems, self.used = sems, 0

    def __call__(self, src, dst):
        copy = pltpu.make_async_copy(src, dst, self.sems.at[self.used])
        self.used += 1
        copy.start()
        return copy

    def all(self, pairs):
        return [self(src, dst) for src, dst in pairs]


def wait(*copies):
    for copy in copies:
        copy.wait()


def normalized(x):
    center = x - jnp.mean(x, axis=-1, keepdims=True)
    rstd = lax.rsqrt(jnp.mean(center * center, axis=-1, keepdims=True) + EPS)
    return center * rstd, rstd


def norm_rows(scal, table, sub_layer):
    return table[jnp.bitwise_xor(scal[3], sub_layer)]


def put_halves(scal, dst, mine, other):
    half = mine.shape[0]
    core = scal[0]
    dst[span(core * half, half), :] = mine[...].astype(F32)
    dst[span((1 - core) * half, half), :] = other[...].astype(F32)


def take_halves(scal, src, mine, other):
    half = mine.shape[0]
    core = scal[0]
    mine[...] = src[span(core * half, half), :].astype(BF16)
    other[...] = src[span((1 - core) * half, half), :].astype(BF16)


def attn_pieces(scal, pieces, dst):
    if len(pieces) == 1:
        return [(pieces[0], dst)]
    own, near, far, direct = pieces
    half, part = own.shape[1], near.shape[0]
    dp, parity = scal[1], scal[2]
    peer = span((1 - dp) * half, half)
    return [
        (own, dst.at[:, span(dp * half, half)]),
        (near, dst.at[span(parity * part, part), peer]),
        (far, dst.at[span((1 - parity) * part, part), peer]),
        (direct, dst.at[pl.ds(2 * part, part), peer]),
    ]


def mlp_pieces(scal, pieces, up, down):
    if len(pieces) == 2:
        return [(pieces[0], up)], [(pieces[1], down)]
    own_up, own_down, near, far, direct = pieces
    half, part = own_up.shape[0], near.shape[0] // 2
    dp, parity = scal[1], scal[2]
    peer = span((1 - dp) * half, half)
    ups = [(own_up, up.at[span(dp * half, half), :])]
    downs = [(own_down, down.at[:, span(dp * half, half)])]
    for piece, index in ((near, parity), (far, 1 - parity), (direct, 2)):
        ups.append(
            (piece.at[pl.ds(0, part), :], up.at[span((1 - dp) * half + index * part, part), :])
        )
        for side in (0, 1):
            downs.append(
                (
                    piece.at[pl.ds(part, part), pl.ds(side * half, half)],
                    down.at[span((2 * index + side) * part, part), peer],
                )
            )
    return ups, downs


def head_mask(width):
    return lax.broadcasted_iota(jnp.int32, (1, width), 1) // HEAD


def only(mask, values):
    return jnp.where(mask, values, jnp.zeros((), values.dtype))


def attn_pack(layer, scal, qkv, out, own, shared, direct, wide, low, sems):
    copy = Copies(sems)
    part = shared.shape[0]
    count = qkv.shape[1]
    rest = count - 2 * part
    loads = []
    for index in (scal[2], 1 - scal[2]):
        here = span(index * part, part)
        loads.append((here, [copy(qkv.at[layer, here], wide.at[here])]))
    loads.append(
        (
            pl.ds(2 * part, part),
            [
                copy(qkv.at[layer, pl.ds(2 * part, rest)], wide.at[pl.ds(2 * part, rest)]),
                copy(out.at[layer], wide.at[pl.ds(count, part - rest)]),
            ],
        )
    )
    keep = []
    for (here, copies), piece in zip(loads, (shared, None, direct)):
        wait(*copies)
        third = wide[here, :].astype(BF16)
        low[here, :] = third
        if piece is not None:
            piece[...] = third
        keep.append(copy(low.at[here], own.at[here]))
    wait(*keep)


def mlp_pack(
    layer, scal, up, down, own_up, own_down, shared, direct, wide_up, wide_down, low_up, low_down,
    sems,
):
    copy = Copies(sems)
    half, part = wide_up.shape[0], shared.shape[0] // 2
    loads = []
    for index in (scal[2], 1 - scal[2], 2):
        here, there = span(index * part, part), span(2 * index * part, 2 * part)
        loads.append(
            (
                here,
                there,
                copy(up.at[layer, here], wide_up.at[here]),
                copy(down.at[layer, there], wide_down.at[there]),
            )
        )
    keep = []
    for (here, there, *copies), piece in zip(loads, (shared, None, direct)):
        wait(*copies)
        third_up, third_down = wide_up[here, :].astype(BF16), wide_down[there, :].astype(BF16)
        low_up[here, :] = third_up
        low_down[there, :] = third_down
        keep.append(copy(low_up.at[here], own_up.at[here]))
        keep.append(copy(low_down.at[there], own_down.at[there]))
        if piece is not None:
            piece[:part, :] = third_up
            piece[part:, :half] = third_down[:part]
            piece[part:, half:] = third_down[part:]
    wait(*keep)


def residual(scal, table, sub_layer, refs, x_out):
    x_prev, mine, other = refs
    put_halves(scal, x_out, mine, other)
    bias = norm_rows(scal, table, sub_layer - 1)[2:3]
    x_out[...] = x_prev[...] + (x_out[...] + bias)
    return x_out[...]


def attn_forward(sub_layer, scal, table, *refs):
    if sub_layer == 0:
        x_ref, refs = refs[0], refs[1:]
    else:
        res, refs = refs[:3], refs[3:]
    (seg_col, seg_row, inner, w), refs = refs[:4], refs[4:]
    if sub_layer:
        x_ref, refs = refs[0], refs[1:]
        residual(scal, table, sub_layer, res, x_ref)
    low_out, qkv_out, soft_out, ctx_out, mine, other, total = refs
    x = x_ref[...]
    xhat, _ = normalized(x)
    norm = norm_rows(scal, table, sub_layer)
    low = (xhat * norm[0:1] + norm[1:2]).astype(BF16)
    low_out[...] = low
    width = ctx_out.shape[1]
    q = (dot_abt(low, w[:width]) + inner[0:1, :]).astype(BF16)
    k = dot_abt(low, w[width : 2 * width]).astype(BF16)
    v = (dot_abt(low, w[2 * width : 3 * width]) + inner[1:2, :]).astype(BF16)
    qkv_out[0] = q
    qkv_out[1] = k
    qkv_out[2] = v
    same = seg_col[...] == seg_row[...]
    heads = head_mask(width)
    context = jnp.zeros((x.shape[0], width), F32)
    for h in range(width // HEAD):
        scores = dot_abt(only(heads == h, q), k) * HEAD ** (-0.5)
        scores = jnp.where(same, scores, MASKED)
        expanded = jnp.exp(scores - jnp.max(scores, axis=-1, keepdims=True))
        soft = expanded / jnp.sum(expanded, axis=-1, keepdims=True)
        soft_out[h] = soft
        context = context + dot_ab(soft.astype(BF16), only(heads == h, v))
    context = context.astype(BF16)
    ctx_out[...] = context
    total[...] = dot_ab(context, w[3 * width :])
    take_halves(scal, total, mine, other)


def mlp_forward(sub_layer, count, scal, table, *refs):
    res, up_bias, up, down, refs = refs[:3], refs[3], refs[4], refs[5], refs[6:]
    if count:
        cotangent, refs = refs[0], refs[1:]
        x_out, mine, other, small, back_mine, back_other = refs[:6]
        grads, (total, full) = refs[6:-2], refs[-2:]
    else:
        x_out, low_out, active_out, slope_out, mine, other, total = refs
    x = residual(scal, table, sub_layer, res, x_out)
    xhat, _ = normalized(x)
    norm = norm_rows(scal, table, sub_layer)
    low = (xhat * norm[0:1] + norm[1:2]).astype(BF16)
    hidden = dot_ab(low, up[...]) + up_bias[...]
    phi = 0.5 * (1.0 + lax.erf(hidden * 0.7071067811865476))
    slope = phi + hidden * (0.3989422804014327 * jnp.exp(-0.5 * hidden * hidden))
    active = (hidden * phi).astype(BF16)
    if count:
        small[...] = jnp.zeros_like(small)
        mlp_back_part(
            scal, count, cotangent[...], low, active, up, down, slope, small, back_mine, back_other,
            grads, total, full,
        )
    else:
        low_out[...] = low
        active_out[...] = active
        slope_out[...] = slope
    total[...] = dot_ab(active, down[...])
    take_halves(scal, total, mine, other)


def norm_backward(scal, table, sub_layer, g_prev, mine, other, x, g_out, small):
    put_halves(scal, g_out, mine, other)
    d_normed = g_out[...]
    xhat, rstd = normalized(x[...])
    small[0:1, :] = jnp.sum(d_normed * xhat, axis=0, keepdims=True)
    small[1:2, :] = jnp.sum(d_normed, axis=0, keepdims=True)
    d_hat = d_normed * norm_rows(scal, table, sub_layer)[0:1]
    inner = jnp.mean(d_hat * xhat, axis=-1, keepdims=True)
    g = g_prev[...] + (d_hat - jnp.mean(d_hat, axis=-1, keepdims=True) - xhat * inner) * rstd
    g_out[...] = g
    return g


def mlp_back_part(
    scal, count, g, low, active, up, down, slope, small, mine, other, grads, total, full
):
    small[2:3, :] = jnp.sum(g, axis=0, keepdims=True)
    g_low = g.astype(BF16)
    full[...] = dot_atb(active, g_low)
    column_halves(scal, full, grads[: len(grads) // 2])
    d_hidden = (dot_abt(g_low, down[...]) * slope).astype(BF16)
    small[3:4, :] = jnp.sum(d_hidden.astype(F32), axis=0, keepdims=True)
    total[...] = dot_abt(d_hidden, up[...])
    take_halves(scal, total, mine, other)
    full[...] = dot_atb(low, d_hidden)
    row_halves(scal, full, grads[len(grads) // 2 :])


def mlp_backward(sub_layer, scal, table, *refs):
    res, (low, active, slope, up, down), refs = refs[:4], refs[4:9], refs[9:]
    g_out, small, mine, other = refs[:4]
    grads, (total, full) = refs[4:-2], refs[-2:]
    small[...] = jnp.zeros_like(small)
    g = norm_backward(scal, table, sub_layer + 1, *res, g_out, small)
    mlp_back_part(
        scal, 0, g, low[...], active[...], up, down, slope[...], small, mine, other, grads, total,
        full,
    )


def attn_backward(sub_layer, scal, table, *refs):
    res, (low, qkv, soft_all, ctx, w), refs = refs[:4], refs[4:9], refs[9:]
    g_out, small, mine, other = refs[:4]
    grads, (total, full) = refs[4:-2], refs[-2:]
    small[...] = jnp.zeros_like(small)
    g = norm_backward(scal, table, sub_layer + 1, *res, g_out, small)
    small[2:3, :] = jnp.sum(g, axis=0, keepdims=True)
    g_low = g.astype(BF16)
    q, k, v = qkv[0], qkv[1], qkv[2]
    width = q.shape[1]
    heads = head_mask(width)
    d_context = dot_abt(g_low, w[3 * width :]).astype(BF16)
    d_q = jnp.zeros(q.shape, F32)
    d_k = jnp.zeros(q.shape, F32)
    d_v = jnp.zeros(q.shape, F32)
    for h in range(width // HEAD):
        soft = soft_all[h]
        d_here = only(heads == h, d_context)
        d_soft = dot_abt(d_here, v)
        d_v = d_v + dot_atb(soft.astype(BF16), d_here)
        weighted = soft * d_soft
        delta = jnp.sum(weighted, axis=-1, keepdims=True)
        d_scores = (weighted - soft * delta).astype(BF16)
        d_q = d_q + dot_ab(d_scores, only(heads == h, k))
        d_k = d_k + dot_atb(d_scores, only(heads == h, q))
    d_q = (d_q * HEAD ** (-0.5)).astype(BF16)
    d_k = (d_k * HEAD ** (-0.5)).astype(BF16)
    d_v = d_v.astype(BF16)
    small[3:4, :width] = jnp.sum(d_q.astype(F32), axis=0, keepdims=True)
    small[4:5, :width] = jnp.sum(d_v.astype(F32), axis=0, keepdims=True)
    total[...] = (
        dot_ab(d_q, w[:width])
        + dot_ab(d_k, w[width : 2 * width])
        + dot_ab(d_v, w[2 * width : 3 * width])
    )
    take_halves(scal, total, mine, other)
    for index, part in enumerate((d_q, d_k, d_v)):
        full[index * width : (index + 1) * width, :] = dot_atb(part, low[...])
    full[3 * width :, :] = dot_atb(ctx[...], g_low)
    column_halves(scal, full, grads)


def output(last, scal, table, x_last, mine, other, out_hbm, token, out, sems):
    token[...] = jnp.zeros_like(token)
    residual(scal, table, last, (x_last, mine, other), out)
    wait(Copies(sems)(out, out_hbm))


def input_backward(scal, table, *refs):
    res, refs = refs[:4], refs[4:]
    g_hbm, small, g_out, sems = refs
    small[...] = jnp.zeros_like(small)
    norm_backward(scal, table, 0, *res, g_out, small)
    wait(Copies(sems)(g_out, g_hbm))


SMALL_ROWS = 16


def input_backward_packed(scal, table, *refs):
    res, smalls, refs = refs[:4], refs[4:8], refs[8:]
    g_hbm, packed, g_out, small, sems = refs
    norm_backward(scal, table, 0, *res, g_out, small)
    keep = Copies(sems)(g_out, g_hbm)
    packed[...] = jnp.zeros_like(packed)
    layers = len(smalls) // 2
    count = 2 * layers
    norms = [small, *smalls]
    for s in range(count):
        packed[s : s + 1, :] = norms[s][0:1, :]
        packed[count + s : count + s + 1, :] = norms[s][1:2, :]
        packed[2 * count + s : 2 * count + s + 1, :] = smalls[s][2:3, :]
    row = 3 * count
    width = packed.shape[1] // (2 * layers)
    for layer in range(layers):
        packed[row + layer : row + layer + 1, :] = smalls[2 * layer + 1][3:4, :]
        for part in range(2):
            lane = (2 * layer + part) * width
            packed[row + layers : row + layers + 1, lane : lane + width] = smalls[2 * layer][
                3 + part : 4 + part, :width
            ]
    wait(keep)


def unpack(layers, scal, held, sent, gain, shift, bias, mlp_bias, attn_bias, packed):
    packed[...] = held[...] + sent[...]
    count = 2 * layers
    for index, out in enumerate((gain, shift, bias)):
        out[...] = packed[pl.ds(index * count + scal[3], 1), :]
    row = 3 * count
    mlp_bias[...] = packed[row : row + layers, :]
    row += layers
    width = attn_bias.shape[1]
    for index in range(attn_bias.shape[0]):
        lane = index * width
        attn_bias[index : index + 1, :] = packed[row : row + 1, lane : lane + width]


def column_halves(scal, full, outs):
    if len(outs) == 1:
        outs[0][...] = full[...].astype(BF16)
        return
    count = len(outs) // 2
    rows, half = outs[0].shape
    for index in range(count):
        own, peer = outs[2 * index], outs[2 * index + 1]
        here = slice(index * rows, (index + 1) * rows)
        own[...] = full[here, span(scal[1] * half, half)].astype(BF16)
        peer[...] = full[here, span((1 - scal[1]) * half, half)].astype(BF16)


def row_halves(scal, full, outs):
    if len(outs) == 1:
        outs[0][...] = full[...].astype(BF16)
        return
    half = outs[0].shape[1]
    for out, index in zip(outs, (scal[1], 1 - scal[1])):
        for side in (0, 1):
            out[side * half : (side + 1) * half, :] = full[
                span(index * half, half), side * half : (side + 1) * half
            ].astype(BF16)


def inner_section(scal):
    return (scal[3] == 1) | (scal[3] == 2)


def pass_kernel(mine, totals, scal, *refs):
    *refs, out = refs
    if not totals:
        out[...] = refs[0][...] + refs[1][...]
        return
    if not mine:
        out[...] = refs[-2][...] + refs[-1][...]
        return

    @pl.when(inner_section(scal))
    def _():
        out[...] = refs[2][...] + refs[3][...]

    @pl.when(jnp.logical_not(inner_section(scal)))
    def _():
        out[...] = refs[0][...] + refs[1][...]


def near_kernel(own, peer, arrived, out):
    out[...] = (own[...] + peer[...]) + arrived[...]


def emit_sums(kind, layer, aliased, scal, held, sent, *refs):
    refs = refs[aliased:]
    *outs, token, wide, sems = refs
    token[...] = jnp.zeros_like(token)
    rows, half = wide.shape

    def put(block):
        if kind == "up":
            for side in (0, 1):
                wide[:, side * rows : (side + 1) * rows] = block[
                    side * rows : (side + 1) * rows, :
                ].astype(F32)
        else:
            wide[...] = block[:rows, :].astype(F32)

    @pl.when(inner_section(scal))
    def _():
        put(held)

    @pl.when(jnp.logical_not(inner_section(scal)))
    def _():
        put(sent)

    copy = Copies(sems)
    copies, row = [], 0
    for out in outs:
        copies.append(copy(wide.at[pl.ds(row, out.shape[1])], out.at[layer]))
        row += out.shape[1]
    wait(*copies)


def shuttle(plan, count, scal, *refs):
    refs, sems = refs[:-1], refs[-1]
    copy = Copies(sems)
    wait(*[copy(src, dst) for src, dst in plan(scal, refs[:count], refs[count:])])


SPACES = {"H": pltpu.HBM, "V": pltpu.VMEM, "W": pltpu.VMEM, "S": pltpu.SMEM, "A": pl.ANY}


def call(body, name, operands, outs, scratch=(), copies=0, aliases=None):
    def shape_of(shape, dtype, place):
        return jax.ShapeDtypeStruct(shape, dtype) if place == "W" else SPACES[place](shape, dtype)

    sems = [pltpu.SemaphoreType.DMA((copies,))] if copies else []
    return pl.pallas_call(
        body,
        out_shape=[shape_of(*out) for out in outs],
        in_specs=[pl.BlockSpec(memory_space=SPACES[place]) for _, place in operands],
        out_specs=[pl.BlockSpec(memory_space=SPACES[place]) for _, _, place in outs],
        scratch_shapes=[pltpu.VMEM(s, d) for s, d in scratch] + sems,
        input_output_aliases=aliases or {},
        compiler_params=pltpu.CompilerParams(vmem_limit_bytes=VMEM_LIMIT),
        cost_estimate=pl.CostEstimate(
            flops=SIDE_COST if name in SIDE else TINY_COST if name in TINY else MAIN_COST,
            bytes_accessed=1000,
            transcendentals=0,
        ),
        name=name,
    )(
        *[
            pltpu.with_memory_space_constraint(array, pltpu.HBM) if place == "H" else array
            for array, place in operands
        ]
    )


def pairs_xor(axis, bit):
    return [(i, i ^ bit) for i in range(lax.axis_size(axis))]


class Order:
    def __init__(self):
        self.tokens = []

    def hold(self, *arrays):
        held = lax.optimization_barrier(tuple(arrays) + tuple(self.tokens))
        self.tokens = list(held)
        return held[: len(arrays)]

    def run(self, body, name, operands, *args, **kwargs):
        tokens, count = self.tokens, len(operands)

        def kernel(*refs):
            body(*refs[:count], *refs[count + len(tokens) :])

        operands = list(operands) + [(token, "A") for token in tokens]
        out = call(kernel, name, operands, *args, **kwargs)
        self.tokens = [out[-1]]
        return out


def add_kernel(held, sent, out):
    out[...] = held[...] + sent[...]


def add(order, held, sent):
    [out] = order.run(
        add_kernel, "add", [(held, "W"), (sent, "W")], [(held.shape, held.dtype, "W")]
    )
    return out


class Pipeline:
    def __init__(self, order, scal, count):
        self.order, self.scal, self.count = order, scal, count
        self.own, self.peer = [], []
        self.passed, self.outer, self.near, self.middle = {}, {}, {}, {}

    def put(self, own, peer):
        self.own.append(own)
        self.peer.append(lax.ppermute(peer, "dp", pairs_xor("dp", 1)))

    def run(self, kernel, name, arrays, scal=()):
        operands = [*scal, *[(array, "W") for array in arrays]]
        return self.order.run(kernel, name, operands, [(arrays[0].shape, BF16, "W")])[0]

    def pass_on(self, t):
        mine = [self.own[t], self.peer[t]] if t < self.count else []
        totals = [self.near[t - 2], self.middle[t - 2]] if t >= 2 else []
        arrays = mine + totals
        kernel = functools.partial(pass_kernel, bool(mine), bool(totals))
        self.passed[t] = self.run(kernel, "add", arrays, [self.scal])
        pairs = ([(0, 1), (3, 2)] if mine else []) + ([(1, 0), (2, 3)] if totals else [])
        self.outer[t] = lax.ppermute(self.passed[t], "section", pairs)

    def across(self, t):
        arrays = [self.own[t], self.peer[t], self.outer[t]]
        self.near[t] = self.run(near_kernel, "add", arrays)
        self.middle[t] = lax.ppermute(self.near[t], "section", [(1, 2), (2, 1)])

    def total(self, t):
        return self.passed[t + 2], self.outer[t + 2]


def shards(
    inputs,
    segments,
    cotangent,
    norm_gain,
    norm_shift,
    out_bias,
    attn_qkv,
    attn_out,
    attn_bias,
    mlp_in,
    mlp_out,
    mlp_bias,
):
    section = lax.axis_index("section")
    dp = lax.axis_index("dp")
    tensor = lax.axis_index("tensor")
    dp_count = lax.axis_size("dp")
    layers = attn_qkv.shape[0]
    rows, model = inputs.shape[2], inputs.shape[3]
    half = rows // 2
    shard = attn_qkv.shape[1]
    width = attn_out.shape[2]
    units = mlp_in.shape[2]
    heads = width // HEAD
    core = tensor % 2
    scal = (jnp.stack([core, dp, section % 2, section]).astype(jnp.int32), "S")
    paired = dp_count == 2
    order = Order()

    def places(place, arrays):
        return [(array, place) for array in arrays]

    table = jnp.concatenate([norm_gain, norm_shift, out_bias], axis=0)
    table = jnp.pad(table, ((0, 5), (0, 0)))[None]
    for bit in (1, 2):
        table = jnp.concatenate([table, lax.ppermute(table, "section", pairs_xor("section", bit))])
    table = (table, "V")

    qkv_t = attn_qkv.transpose(0, 2, 3, 1).reshape(layers, 3 * width, shard)
    out_t = attn_out.transpose(0, 2, 1)

    def sent(shared, direct):
        near = lax.ppermute(shared, "dp", pairs_xor("dp", 1))
        return [near, None, lax.ppermute(direct, "dp", pairs_xor("dp", 1))]

    def send_on(weights):
        if paired:
            [weights[-3]] = order.hold(weights[-3])
            weights[-2] = lax.ppermute(weights[-3], "section", pairs_xor("section", 1))

    def arrived(weights):
        if paired:
            [weights[-1]] = order.hold(weights[-1])

    def attn_gather(layer):
        if not paired:
            pack = jnp.concatenate([qkv_t[layer], out_t[layer]], axis=0).astype(BF16)
            return [lax.all_gather(pack, "dp", axis=1, tiled=True)]
        third = 4 * width // 3
        own, shared, direct = order.run(
            functools.partial(attn_pack, layer),
            "attn_pack",
            [scal, (qkv_t, "H"), (out_t, "H")],
            [((4 * width, shard), BF16, "H")] + [((third, shard), BF16, "V")] * 2,
            [((4 * width, shard), F32), ((4 * width, shard), BF16)],
            copies=7,
        )
        return [own, *sent(shared, direct)]

    def mlp_gather(layer):
        if not paired:
            return [
                lax.all_gather(mlp_in[layer].astype(BF16), "dp", axis=0, tiled=True),
                lax.all_gather(mlp_out[layer].astype(BF16), "dp", axis=1, tiled=True),
            ]
        third = 2 * shard // 3
        own_up, own_down, shared, direct = order.run(
            functools.partial(mlp_pack, layer),
            "mlp_pack",
            [scal, (mlp_in, "H"), (mlp_out, "H")],
            [((shard, units), BF16, "H"), ((units, shard), BF16, "H")]
            + [((third, units), BF16, "V")] * 2,
            [(shape, kind) for kind in (F32, BF16) for shape in ((shard, units), (units, shard))],
            copies=12,
        )
        return [own_up, own_down, *sent(shared, direct)]

    seg = lax.dynamic_index_in_dim(segments[:, 0], section, 0, keepdims=False)
    segs = [(seg[:, None], "V"), (seg[None, :], "V")]

    row_f32, row_low = ((rows, model), F32), ((rows, model), BF16)
    unit_f32, unit_low = ((rows, units), F32), ((rows, units), BF16)
    half_low = ((half, model), BF16)
    small_out = ((8, model), F32, "W")
    qkv_low, soft_f32 = ((3, rows, width), BF16), ((heads, rows, rows), F32)
    ctx_low, attn_full = ((rows, width), BF16), ((4 * width, model), BF16)
    up_full, down_full = ((model, units), BF16), ((units, model), BF16)

    def held(*shapes):
        return [shape + ("V",) for shape in shapes]

    def move_data(save=(), fetch=(), attn=None, mlp=None):
        pieces = attn or mlp or []

        def plan(scal, ins, outs):
            count = len(save) + len(fetch)
            pairs = list(zip(ins[:count], outs[:count]))
            if attn:
                pairs += attn_pieces(scal, ins[count:], outs[count])
            if mlp:
                ups, downs = mlp_pieces(scal, ins[count:], *outs[count:])
                pairs += ups + downs
            return pairs

        outs = [(array.shape, array.dtype, "H") for array in save]
        outs += [(array.shape, array.dtype, "V") for array in fetch]
        outs += held(attn_full) if attn else held(up_full, down_full) if mlp else []
        operands = places("V", save) + places("H", list(fetch) + list(pieces))
        return order.run(
            functools.partial(shuttle, plan, len(operands)),
            "shuttle",
            [scal, *operands],
            outs,
            copies=len(save) + len(fetch) + (11 if mlp else 4),
        )

    def nothing():
        return None

    def tensor_sum(mine, other, window=nothing, ahead=nothing, moves=((), (), ())):
        arrived = lax.ppermute(other, "tensor", pairs_xor("tensor", 1))
        ahead()
        move(*moves[0])
        near = add(order, mine, arrived)
        arrived = lax.ppermute(near, "tensor", pairs_xor("tensor", 2))
        window()
        move(*moves[1])
        total = add(order, near, arrived)
        arrived = lax.ppermute(total, "tensor", pairs_xor("tensor", 1))
        move(*moves[2])
        return [total, arrived]

    def fore_steps(mine, other):
        arrived = lax.ppermute(other, "tensor", pairs_xor("tensor", 1))
        yield
        near = add(order, mine, arrived)
        arrived = lax.ppermute(near, "tensor", pairs_xor("tensor", 2))
        yield
        total = add(order, near, arrived)
        arrived = lax.ppermute(total, "tensor", pairs_xor("tensor", 1))
        yield
        out, _ = order.run(
            functools.partial(output, 2 * layers),
            "output",
            [scal, table, *places("V", [x3, total, arrived])],
            [row_f32 + ("H",), ((8, 128), F32, "V")],
            [row_f32],
            copies=1,
        )
        yield out

    def attn_step(s, res, w):
        return order.run(
            functools.partial(attn_forward, s),
            "attn_forward",
            [scal, table, *places("V", res), *segs, *places("V", [attn_bias[s // 2], w])],
            held(*([row_f32] if s else []), row_low, qkv_low, soft_f32, ctx_low, half_low, half_low),
            [row_f32],
        )

    def mlp_step(s, res, up, down, cotangent=None):
        last = cotangent is not None
        operands = [*res, mlp_bias[s // 2][None], up, down] + ([cotangent] if last else [])
        if last:
            grads = mlp_shapes()
            outs = held(row_f32, half_low, half_low) + [small_out] + held(half_low, half_low)
            outs += grads
        else:
            grads = []
            outs = held(row_f32, row_low, unit_low, unit_f32, half_low, half_low)
        return order.run(
            functools.partial(mlp_forward, s, len(grads)),
            "mlp_forward",
            [scal, table, *places("V", operands)],
            outs,
            [row_f32] + ([(up_full[0], F32)] if last else []),
        )

    def mlp_shapes():
        if not paired:
            return [(down_full[0], BF16, "W"), (up_full[0], BF16, "W")]
        return [((units, shard), BF16, "W")] * 4

    def attn_shapes():
        if not paired:
            return [(attn_full[0], BF16, "W")]
        return [((4 * width, shard), BF16, "W")] * 2

    chunks = []
    pipeline = Pipeline(order, scal, 3 * layers)

    def add_chunks(parts, axis):
        if not paired:
            whole = lax.psum_scatter(parts[0], "dp", scatter_dimension=axis, tiled=True)
            chunks.append(lax.psum(whole, "section"))
            return
        for own, peer in zip(parts[0::2], parts[1::2]):
            pipeline.put(own, peer)

    emitted = {}

    def emit(kind, layer, index):
        shape = {"up": (shard, units), "down": (units, shard), "attn": (4 * width, shard)}[kind]
        token = ((8, 128), F32, "V")
        outs = [((layers,) + shape, F32, "H")]
        if kind == "attn":
            outs = [((layers, count, shard), F32, "H") for count in (3 * width, width)]
        before = emitted.get(kind, [])
        operands = list(pipeline.total(index))
        *emitted[kind], _ = order.run(
            functools.partial(emit_sums, kind, layer, len(before)),
            "emit",
            [scal, *places("W", operands), *places("H", before)],
            [*outs, token],
            [(shape, F32)],
            copies=2,
            aliases={1 + len(operands) + index: index for index in range(len(before))},
        )

    def small_sum(held):
        sent = lax.ppermute(held, "dp", pairs_xor("dp", 1))
        for bit in (1, 2):
            yield
            held = add(order, held, sent)
            sent = lax.ppermute(held, "section", pairs_xor("section", bit))
        yield
        yield order.run(
            functools.partial(unpack, layers),
            "unpack",
            [scal, (held, "W"), (sent, "W")],
            [((1, model), F32, "W")] * 3
            + [((layers, units), F32, "W"), ((2 * layers, width), F32, "W")],
            [((SMALL_ROWS, model), F32)],
        )

    def move(*indices):
        for index in indices:
            if index == FORE:
                fore.append(next(fore[0]))
            elif index == SMALL:
                small_steps.append(next(small_steps[0]))
            elif not paired:
                continue
            else:
                step, t = index
                if step == EMIT:
                    emit(("down", "up", "attn")[t % 3], layers - 1 - t // 3, t)
                else:
                    (pipeline.pass_on if step == PASS else pipeline.across)(t)

    def mlp_chunks(parts):
        add_chunks(parts[: len(parts) // 2], 1)
        add_chunks(parts[len(parts) // 2 :], 0)

    def back(body, name, s, operands, full, grads):
        return order.run(
            functools.partial(body, s),
            name,
            [scal, table, *places("V", operands)],
            held(row_f32) + [small_out] + held(half_low, half_low) + grads,
            [row_f32, (full[0], F32)],
        )

    box = {}

    def keep(names, values):
        box.update(zip(names, values))

    def kept(*names):
        return [box[name] for name in names]

    x0 = inputs.reshape(rows, model)
    pieces = {}

    def weigh(*steps):
        for step, s in steps:
            if step == PACK:
                pieces[s] = (mlp_gather if s % 2 else attn_gather)(s // 2)
            else:
                (send_on if step == ON else arrived)(pieces[s])

    weigh(*WEIGHTS[0])
    [w] = move_data(attn=pieces[0])
    low, qkv, soft, ctx, *halves = attn_step(0, [x0], w)

    def window():
        weigh(*WEIGHTS[2])
        keep(
            ("low0", "qkv0", "soft0", "ctx0", "up", "down"),
            move_data([low, qkv, soft, ctx], mlp=pieces[1]),
        )
        weigh(*WEIGHTS[3])

    total = tensor_sum(*halves, window, lambda: weigh(*WEIGHTS[1]))
    x1, low, active, slope, *halves = mlp_step(1, [x0, *total], box["up"], box["down"])

    def window():
        weigh(*WEIGHTS[5])
        keep(
            ("x1", "low1", "active1", "slope1", "w"),
            move_data([x1, low, active, slope], attn=pieces[2]),
        )
        weigh(*WEIGHTS[6])

    total = tensor_sum(*halves, window, lambda: weigh(*WEIGHTS[4]))
    x2, low, qkv, soft, ctx, *halves = attn_step(2, [x1, *total], box["w"])

    def window():
        weigh(*WEIGHTS[8])
        keep(
            ("x2", "low2", "qkv2", "soft2", "ctx2", "up", "down"),
            move_data([x2, low, qkv, soft, ctx], mlp=pieces[3]),
        )

    total = tensor_sum(*halves, window, lambda: weigh(*WEIGHTS[7]))
    g = cotangent.reshape(rows, model)
    x3, fore_mine, fore_other, small3, *rest = mlp_step(
        3, [x2, *total], box["up"], box["down"], g
    )
    fore = [fore_steps(fore_mine, fore_other)]

    def window():
        keep(
            ("low", "ctx", "qkv", "soft", "w"),
            move_data(fetch=kept("low2", "ctx2", "qkv2", "soft2"), attn=pieces[2]),
        )

    total = tensor_sum(*rest[:2], window, lambda: mlp_chunks(rest[2:]), MOVES[0])
    operands = [g, *total, x3, *kept("low", "qkv", "soft", "ctx", "w")]
    g, small2, *rest = back(
        attn_backward, "attn_backward", 2, operands, attn_full, attn_shapes()
    )

    def window():
        keep(
            ("x", "low", "active", "slope", "up", "down"),
            move_data(fetch=kept("x2", "low1", "active1", "slope1"), mlp=pieces[1]),
        )

    total = tensor_sum(*rest[:2], window, lambda: add_chunks(rest[2:], 1), MOVES[1])
    operands = [g, *total, *kept("x", "low", "active", "slope", "up", "down")]
    g, small1, *rest = back(mlp_backward, "mlp_backward", 1, operands, up_full, mlp_shapes())

    def window():
        keep(
            ("x", "low", "ctx", "qkv", "soft", "w"),
            move_data(fetch=kept("x1", "low0", "ctx0", "qkv0", "soft0"), attn=pieces[0]),
        )

    total = tensor_sum(*rest[:2], window, lambda: mlp_chunks(rest[2:]), MOVES[2])
    operands = [g, *total, *kept("x", "low", "qkv", "soft", "ctx", "w")]
    g, small0, *rest = back(
        attn_backward, "attn_backward", 0, operands, attn_full, attn_shapes()
    )
    total = tensor_sum(*rest[:2], ahead=lambda: add_chunks(rest[2:], 1), moves=MOVES[3])
    operands = [g, *total, x0]
    if paired:
        input_grad, small = order.run(
            input_backward_packed,
            "input_backward",
            [scal, table, *places("V", [*operands, small0, small1, small2, small3])],
            [row_f32 + ("H",), ((SMALL_ROWS, model), F32, "W")],
            [row_f32, ((8, model), F32)],
            copies=1,
        )
        small_steps = [small_sum(small)]
        move(*MOVES[4])
        [up_grad], [down_grad], (qkv_grad, out_grad) = (
            emitted[kind] for kind in ("up", "down", "attn")
        )
        gain_grad, shift_grad, bias_grad, mlp_rows, attn_rows = small_steps[4]
        attn_rows = attn_rows.reshape(layers, 2, width)
    else:
        input_grad, small = order.run(
            input_backward,
            "input_backward",
            [scal, table, *places("V", operands)],
            [row_f32 + ("H",), small_out],
            [row_f32],
            copies=1,
        )
        small = jnp.stack([small, small0, small1, small2, small3])
        small = lax.psum(small, ("section", "dp"))
        down_grad, up_grad, pack = [
            jnp.stack(chunks[3 + kind :: -3]).astype(F32) for kind in range(3)
        ]
        qkv_grad, out_grad = pack[:, : 3 * width], pack[:, 3 * width :]
        gain_grad, shift_grad, bias_grad = [
            lax.dynamic_slice_in_dim(rows_all, section, 1, 0)
            for rows_all in (small[:-1, 0], small[:-1, 1], small[1:, 2])
        ]
        mlp_rows = jnp.stack([small[2 * layer + 2, 3, :units] for layer in range(layers)])
        attn_rows = jnp.stack([small[2 * layer + 1, 3:5, :width] for layer in range(layers)])
    while len(fore) < 5:
        move(FORE)
    outputs = fore[4]
    qkv_grad = qkv_grad.reshape(layers, 3, width, shard).transpose(0, 3, 1, 2)

    return (
        outputs.reshape(inputs.shape),
        input_grad.reshape(inputs.shape),
        gain_grad,
        shift_grad,
        bias_grad,
        qkv_grad,
        out_grad.transpose(0, 2, 1),
        attn_rows,
        up_grad,
        down_grad,
        mlp_rows,
    )


def solution(mesh):
    placed = (
        P("section", "dp", None, None),
        P(None, "dp", None),
        P("section", "dp", None, None),
        P("section", None),
        P("section", None),
        P("section", None),
        P(None, "dp", None, "tensor"),
        P(None, "dp", "tensor"),
        P(None, None, "tensor"),
        P(None, "dp", "tensor"),
        P(None, "tensor", "dp"),
        P(None, "tensor"),
    )
    return jax.shard_map(
        shards,
        mesh=mesh,
        in_specs=placed,
        out_specs=(
            P("section", "dp", None, None),
            P("section", "dp", None, None),
            P("section", None),
            P("section", None),
            P("section", None),
            P(None, "dp", None, "tensor"),
            P(None, "dp", "tensor"),
            P(None, None, "tensor"),
            P(None, "dp", "tensor"),
            P(None, "tensor", "dp"),
            P(None, "tensor"),
        ),
        check_vma=False,
    )
```

```python
import functools

import jax
import jax.numpy as jnp
from jax import lax
from jax.experimental import pallas as pl
from jax.experimental.pallas import tpu as pltpu
from jax.sharding import PartitionSpec as P

HEAD = 64
EPS = 1e-06
MASKED = -1e30
BF16 = jnp.bfloat16
F32 = jnp.float32
VMEM_LIMIT = 12 * 1024 * 1024
SIDE = ("shuttle", "attn_pack", "mlp_pack")
TINY = ("add", "emit")


def dot_ab(a, b):
    return lax.dot_general(a, b, (((1,), (0,)), ((), ())), preferred_element_type=F32)


def dot_abt(a, b):
    return lax.dot_general(a, b, (((1,), (1,)), ((), ())), preferred_element_type=F32)


def dot_atb(a, b):
    return lax.dot_general(a, b, (((0,), (0,)), ((), ())), preferred_element_type=F32)


SIDE_COST, MAIN_COST, TINY_COST = 1000, 1000, 1000
PASS, ACROSS, EMIT, FORE, SMALL = 0, 1, 2, 3, 4
MOVES = (
    ((FORE,), (), ()),
    (((PASS, 0),), (FORE,), ()),
    (((PASS, 1), (ACROSS, 0), FORE), ((PASS, 2),), ((ACROSS, 1), FORE)),
    (((PASS, 3),), ((ACROSS, 2), (EMIT, 0)), ((PASS, 4), (ACROSS, 3), (EMIT, 1))),
    (SMALL, (PASS, 5), (ACROSS, 4), (EMIT, 2), SMALL, (PASS, 6), (ACROSS, 5), (EMIT, 3), SMALL, (EMIT, 4), (PASS, 7), SMALL, (EMIT, 5)),
)
PACK, ON, BY = 0, 1, 2
WEIGHTS = (
    ((PACK, 0), (PACK, 1), (ON, 0), (PACK, 2)),
    ((ON, 1), (PACK, 3)),
    (),
    ((BY, 2),),
    ((ON, 2),),
    (),
    ((ON, 3),),
    (),
    ((BY, 3),),
)


def span(start, size):
    return pl.ds(pl.multiple_of(start, size), size)


class Copies:
    def __init__(self, sems):
        self.sems, self.used = sems, 0

    def __call__(self, src, dst):
        copy = pltpu.make_async_copy(src, dst, self.sems.at[self.used])
        self.used += 1
        copy.start()
        return copy

    def all(self, pairs):
        return [self(src, dst) for src, dst in pairs]


def wait(*copies):
    for copy in copies:
        copy.wait()


def normalized(x):
    center = x - jnp.mean(x, axis=-1, keepdims=True)
    rstd = lax.rsqrt(jnp.mean(center * center, axis=-1, keepdims=True) + EPS)
    return center * rstd, rstd


def norm_rows(scal, table, sub_layer):
    return table[jnp.bitwise_xor(scal[3], sub_layer)]


def put_halves(scal, dst, mine, other):
    half = mine.shape[0]
    core = scal[0]
    dst[span(core * half, half), :] = mine[...].astype(F32)
    dst[span((1 - core) * half, half), :] = other[...].astype(F32)


def take_halves(scal, src, mine, other):
    half = mine.shape[0]
    core = scal[0]
    mine[...] = src[span(core * half, half), :].astype(BF16)
    other[...] = src[span((1 - core) * half, half), :].astype(BF16)


def attn_pieces(scal, pieces, dst):
    if len(pieces) == 1:
        return [(pieces[0], dst)]
    own, near, far, direct = pieces
    half, part = own.shape[1], near.shape[0]
    dp, parity = scal[1], scal[2]
    peer = span((1 - dp) * half, half)
    return [
        (own, dst.at[:, span(dp * half, half)]),
        (near, dst.at[span(parity * part, part), peer]),
        (far, dst.at[span((1 - parity) * part, part), peer]),
        (direct, dst.at[pl.ds(2 * part, part), peer]),
    ]


def mlp_pieces(scal, pieces, up, down):
    if len(pieces) == 2:
        return [(pieces[0], up)], [(pieces[1], down)]
    own_up, own_down, near, far, direct = pieces
    half, part = own_up.shape[0], near.shape[0] // 2
    dp, parity = scal[1], scal[2]
    peer = span((1 - dp) * half, half)
    ups = [(own_up, up.at[span(dp * half, half), :])]
    downs = [(own_down, down.at[:, span(dp * half, half)])]
    for piece, index in ((near, parity), (far, 1 - parity), (direct, 2)):
        ups.append(
            (piece.at[pl.ds(0, part), :], up.at[span((1 - dp) * half + index * part, part), :])
        )
        for side in (0, 1):
            downs.append(
                (
                    piece.at[pl.ds(part, part), pl.ds(side * half, half)],
                    down.at[span((2 * index + side) * part, part), peer],
                )
            )
    return ups, downs


def head_mask(width):
    return lax.broadcasted_iota(jnp.int32, (1, width), 1) // HEAD


def only(mask, values):
    return jnp.where(mask, values, jnp.zeros((), values.dtype))


def attn_pack(layer, scal, qkv, out, own, shared, direct, wide, low, sems):
    copy = Copies(sems)
    part = shared.shape[0]
    count = qkv.shape[1]
    rest = count - 2 * part
    loads = []
    for index in (scal[2], 1 - scal[2]):
        here = span(index * part, part)
        loads.append((here, [copy(qkv.at[layer, here], wide.at[here])]))
    loads.append(
        (
            pl.ds(2 * part, part),
            [
                copy(qkv.at[layer, pl.ds(2 * part, rest)], wide.at[pl.ds(2 * part, rest)]),
                copy(out.at[layer], wide.at[pl.ds(count, part - rest)]),
            ],
        )
    )
    keep = []
    for (here, copies), piece in zip(loads, (shared, None, direct)):
        wait(*copies)
        third = wide[here, :].astype(BF16)
        low[here, :] = third
        if piece is not None:
            piece[...] = third
        keep.append(copy(low.at[here], own.at[here]))
    wait(*keep)


def mlp_pack(
    layer, scal, up, down, own_up, own_down, shared, direct, wide_up, wide_down, low_up, low_down,
    sems,
):
    copy = Copies(sems)
    half, part = wide_up.shape[0], shared.shape[0] // 2
    loads = []
    for index in (scal[2], 1 - scal[2], 2):
        here, there = span(index * part, part), span(2 * index * part, 2 * part)
        loads.append(
            (
                here,
                there,
                copy(up.at[layer, here], wide_up.at[here]),
                copy(down.at[layer, there], wide_down.at[there]),
            )
        )
    keep = []
    for (here, there, *copies), piece in zip(loads, (shared, None, direct)):
        wait(*copies)
        third_up, third_down = wide_up[here, :].astype(BF16), wide_down[there, :].astype(BF16)
        low_up[here, :] = third_up
        low_down[there, :] = third_down
        keep.append(copy(low_up.at[here], own_up.at[here]))
        keep.append(copy(low_down.at[there], own_down.at[there]))
        if piece is not None:
            piece[:part, :] = third_up
            piece[part:, :half] = third_down[:part]
            piece[part:, half:] = third_down[part:]
    wait(*keep)


def residual(scal, table, sub_layer, refs, x_out):
    x_prev, mine, other = refs
    put_halves(scal, x_out, mine, other)
    bias = norm_rows(scal, table, sub_layer - 1)[2:3]
    x_out[...] = x_prev[...] + (x_out[...] + bias)
    return x_out[...]


def attn_forward(sub_layer, scal, table, *refs):
    if sub_layer == 0:
        x_ref, refs = refs[0], refs[1:]
    else:
        res, refs = refs[:3], refs[3:]
    (seg_col, seg_row, inner, w), refs = refs[:4], refs[4:]
    if sub_layer:
        x_ref, refs = refs[0], refs[1:]
        residual(scal, table, sub_layer, res, x_ref)
    low_out, qkv_out, soft_out, ctx_out, mine, other, total = refs
    x = x_ref[...]
    xhat, _ = normalized(x)
    norm = norm_rows(scal, table, sub_layer)
    low = (xhat * norm[0:1] + norm[1:2]).astype(BF16)
    low_out[...] = low
    width = ctx_out.shape[1]
    q = (dot_abt(low, w[:width]) + inner[0:1, :]).astype(BF16)
    k = dot_abt(low, w[width : 2 * width]).astype(BF16)
    v = (dot_abt(low, w[2 * width : 3 * width]) + inner[1:2, :]).astype(BF16)
    qkv_out[0] = q
    qkv_out[1] = k
    qkv_out[2] = v
    same = seg_col[...] == seg_row[...]
    heads = head_mask(width)
    context = jnp.zeros((x.shape[0], width), F32)
    for h in range(width // HEAD):
        scores = dot_abt(only(heads == h, q), k) * HEAD ** (-0.5)
        scores = jnp.where(same, scores, MASKED)
        expanded = jnp.exp(scores - jnp.max(scores, axis=-1, keepdims=True))
        soft = expanded / jnp.sum(expanded, axis=-1, keepdims=True)
        soft_out[h] = soft
        context = context + dot_ab(soft.astype(BF16), only(heads == h, v))
    context = context.astype(BF16)
    ctx_out[...] = context
    total[...] = dot_ab(context, w[3 * width :])
    take_halves(scal, total, mine, other)


def mlp_forward(sub_layer, count, scal, table, *refs):
    res, up_bias, up, down, refs = refs[:3], refs[3], refs[4], refs[5], refs[6:]
    if count:
        cotangent, refs = refs[0], refs[1:]
        x_out, mine, other, small, back_mine, back_other = refs[:6]
        grads, (total, full) = refs[6:-2], refs[-2:]
    else:
        x_out, low_out, active_out, slope_out, mine, other, total = refs
    x = residual(scal, table, sub_layer, res, x_out)
    xhat, _ = normalized(x)
    norm = norm_rows(scal, table, sub_layer)
    low = (xhat * norm[0:1] + norm[1:2]).astype(BF16)
    hidden = dot_ab(low, up[...]) + up_bias[...]
    phi = 0.5 * (1.0 + lax.erf(hidden * 0.7071067811865476))
    slope = phi + hidden * (0.3989422804014327 * jnp.exp(-0.5 * hidden * hidden))
    active = (hidden * phi).astype(BF16)
    if count:
        small[...] = jnp.zeros_like(small)
        mlp_back_part(
            scal, count, cotangent[...], low, active, up, down, slope, small, back_mine, back_other,
            grads, total, full,
        )
    else:
        low_out[...] = low
        active_out[...] = active
        slope_out[...] = slope
    total[...] = dot_ab(active, down[...])
    take_halves(scal, total, mine, other)


def norm_backward(scal, table, sub_layer, g_prev, mine, other, x, g_out, small):
    put_halves(scal, g_out, mine, other)
    d_normed = g_out[...]
    xhat, rstd = normalized(x[...])
    small[0:1, :] = jnp.sum(d_normed * xhat, axis=0, keepdims=True)
    small[1:2, :] = jnp.sum(d_normed, axis=0, keepdims=True)
    d_hat = d_normed * norm_rows(scal, table, sub_layer)[0:1]
    inner = jnp.mean(d_hat * xhat, axis=-1, keepdims=True)
    g = g_prev[...] + (d_hat - jnp.mean(d_hat, axis=-1, keepdims=True) - xhat * inner) * rstd
    g_out[...] = g
    return g


def mlp_back_part(
    scal, count, g, low, active, up, down, slope, small, mine, other, grads, total, full
):
    small[2:3, :] = jnp.sum(g, axis=0, keepdims=True)
    g_low = g.astype(BF16)
    full[...] = dot_atb(active, g_low)
    column_halves(scal, full, grads[: len(grads) // 2])
    d_hidden = (dot_abt(g_low, down[...]) * slope).astype(BF16)
    small[3:4, :] = jnp.sum(d_hidden.astype(F32), axis=0, keepdims=True)
    total[...] = dot_abt(d_hidden, up[...])
    take_halves(scal, total, mine, other)
    full[...] = dot_atb(low, d_hidden)
    row_halves(scal, full, grads[len(grads) // 2 :])


def mlp_backward(sub_layer, scal, table, *refs):
    res, (low, active, slope, up, down), refs = refs[:4], refs[4:9], refs[9:]
    g_out, small, mine, other = refs[:4]
    grads, (total, full) = refs[4:-2], refs[-2:]
    small[...] = jnp.zeros_like(small)
    g = norm_backward(scal, table, sub_layer + 1, *res, g_out, small)
    mlp_back_part(
        scal, 0, g, low[...], active[...], up, down, slope[...], small, mine, other, grads, total,
        full,
    )


def attn_backward(sub_layer, scal, table, *refs):
    res, (low, qkv, soft_all, ctx, w), refs = refs[:4], refs[4:9], refs[9:]
    g_out, small, mine, other = refs[:4]
    grads, (total, full) = refs[4:-2], refs[-2:]
    small[...] = jnp.zeros_like(small)
    g = norm_backward(scal, table, sub_layer + 1, *res, g_out, small)
    small[2:3, :] = jnp.sum(g, axis=0, keepdims=True)
    g_low = g.astype(BF16)
    q, k, v = qkv[0], qkv[1], qkv[2]
    width = q.shape[1]
    heads = head_mask(width)
    d_context = dot_abt(g_low, w[3 * width :]).astype(BF16)
    d_q = jnp.zeros(q.shape, F32)
    d_k = jnp.zeros(q.shape, F32)
    d_v = jnp.zeros(q.shape, F32)
    for h in range(width // HEAD):
        soft = soft_all[h]
        d_here = only(heads == h, d_context)
        d_soft = dot_abt(d_here, v)
        d_v = d_v + dot_atb(soft.astype(BF16), d_here)
        weighted = soft * d_soft
        delta = jnp.sum(weighted, axis=-1, keepdims=True)
        d_scores = (weighted - soft * delta).astype(BF16)
        d_q = d_q + dot_ab(d_scores, only(heads == h, k))
        d_k = d_k + dot_atb(d_scores, only(heads == h, q))
    d_q = (d_q * HEAD ** (-0.5)).astype(BF16)
    d_k = (d_k * HEAD ** (-0.5)).astype(BF16)
    d_v = d_v.astype(BF16)
    small[3:4, :width] = jnp.sum(d_q.astype(F32), axis=0, keepdims=True)
    small[4:5, :width] = jnp.sum(d_v.astype(F32), axis=0, keepdims=True)
    total[...] = (
        dot_ab(d_q, w[:width])
        + dot_ab(d_k, w[width : 2 * width])
        + dot_ab(d_v, w[2 * width : 3 * width])
    )
    take_halves(scal, total, mine, other)
    for index, part in enumerate((d_q, d_k, d_v)):
        full[index * width : (index + 1) * width, :] = dot_atb(part, low[...])
    full[3 * width :, :] = dot_atb(ctx[...], g_low)
    column_halves(scal, full, grads)


def output(last, scal, table, x_last, mine, other, out_hbm, token, out, sems):
    token[...] = jnp.zeros_like(token)
    residual(scal, table, last, (x_last, mine, other), out)
    wait(Copies(sems)(out, out_hbm))


def input_backward(scal, table, *refs):
    res, refs = refs[:4], refs[4:]
    g_hbm, small, g_out, sems = refs
    small[...] = jnp.zeros_like(small)
    norm_backward(scal, table, 0, *res, g_out, small)
    wait(Copies(sems)(g_out, g_hbm))


SMALL_ROWS = 16


def input_backward_packed(scal, table, *refs):
    res, smalls, refs = refs[:4], refs[4:8], refs[8:]
    g_hbm, packed, g_out, small, sems = refs
    norm_backward(scal, table, 0, *res, g_out, small)
    keep = Copies(sems)(g_out, g_hbm)
    packed[...] = jnp.zeros_like(packed)
    layers = len(smalls) // 2
    count = 2 * layers
    norms = [small, *smalls]
    for s in range(count):
        packed[s : s + 1, :] = norms[s][0:1, :]
        packed[count + s : count + s + 1, :] = norms[s][1:2, :]
        packed[2 * count + s : 2 * count + s + 1, :] = smalls[s][2:3, :]
    row = 3 * count
    width = packed.shape[1] // (2 * layers)
    for layer in range(layers):
        packed[row + layer : row + layer + 1, :] = smalls[2 * layer + 1][3:4, :]
        for part in range(2):
            lane = (2 * layer + part) * width
            packed[row + layers : row + layers + 1, lane : lane + width] = smalls[2 * layer][
                3 + part : 4 + part, :width
            ]
    wait(keep)


def unpack(layers, scal, held, sent, gain, shift, bias, mlp_bias, attn_bias, packed):
    packed[...] = held[...] + sent[...]
    count = 2 * layers
    for index, out in enumerate((gain, shift, bias)):
        out[...] = packed[pl.ds(index * count + scal[3], 1), :]
    row = 3 * count
    mlp_bias[...] = packed[row : row + layers, :]
    row += layers
    width = attn_bias.shape[1]
    for index in range(attn_bias.shape[0]):
        lane = index * width
        attn_bias[index : index + 1, :] = packed[row : row + 1, lane : lane + width]


def column_halves(scal, full, outs):
    if len(outs) == 1:
        outs[0][...] = full[...].astype(BF16)
        return
    count = len(outs) // 2
    rows, half = outs[0].shape
    for index in range(count):
        own, peer = outs[2 * index], outs[2 * index + 1]
        here = slice(index * rows, (index + 1) * rows)
        own[...] = full[here, span(scal[1] * half, half)].astype(BF16)
        peer[...] = full[here, span((1 - scal[1]) * half, half)].astype(BF16)


def row_halves(scal, full, outs):
    if len(outs) == 1:
        outs[0][...] = full[...].astype(BF16)
        return
    half = outs[0].shape[1]
    for out, index in zip(outs, (scal[1], 1 - scal[1])):
        for side in (0, 1):
            out[side * half : (side + 1) * half, :] = full[
                span(index * half, half), side * half : (side + 1) * half
            ].astype(BF16)


def inner_section(scal):
    return (scal[3] == 1) | (scal[3] == 2)


def pass_kernel(mine, totals, scal, *refs):
    *refs, out = refs
    if not totals:
        out[...] = refs[0][...] + refs[1][...]
        return
    if not mine:
        out[...] = refs[-2][...] + refs[-1][...]
        return

    @pl.when(inner_section(scal))
    def _():
        out[...] = refs[2][...] + refs[3][...]

    @pl.when(jnp.logical_not(inner_section(scal)))
    def _():
        out[...] = refs[0][...] + refs[1][...]


def near_kernel(own, peer, arrived, out):
    out[...] = (own[...] + peer[...]) + arrived[...]


def emit_sums(kind, layer, aliased, scal, held, sent, *refs):
    refs = refs[aliased:]
    *outs, token, wide, sems = refs
    token[...] = jnp.zeros_like(token)
    copy = Copies(sems)
    rows, half = held.shape[0] // 2, held.shape[1]
    parts = []
    if kind == "up":
        for side in (0, 1):
            lanes = pl.ds(side * half, half)
            parts.append((side * rows, rows, (slice(None), lanes), outs[0].at[layer, :, lanes]))
    else:
        edges = [0, rows, 2 * rows]
        if kind == "attn":
            edges.insert(2, outs[0].shape[1])
        for start, end in zip(edges, edges[1:]):
            first = start < outs[0].shape[1]
            out, base = (outs[0], 0) if first else (outs[1], outs[0].shape[1])
            here = pl.ds(start, end - start)
            target = out.at[layer, pl.ds(start - base, end - start)]
            parts.append((start, end - start, (here, slice(None)), target))
    copies = []
    for start, size, place, target in parts:

        @pl.when(inner_section(scal))
        def _():
            wide[place] = held[start : start + size, :].astype(F32)

        @pl.when(jnp.logical_not(inner_section(scal)))
        def _():
            wide[place] = sent[start : start + size, :].astype(F32)

        copies.append(copy(wide.at[place], target))
    wait(*copies)


def shuttle(plan, count, scal, *refs):
    refs, sems = refs[:-1], refs[-1]
    copy = Copies(sems)
    wait(*[copy(src, dst) for src, dst in plan(scal, refs[:count], refs[count:])])


SPACES = {"H": pltpu.HBM, "V": pltpu.VMEM, "W": pltpu.VMEM, "S": pltpu.SMEM, "A": pl.ANY}


def call(body, name, operands, outs, scratch=(), copies=0, aliases=None):
    def shape_of(shape, dtype, place):
        return jax.ShapeDtypeStruct(shape, dtype) if place == "W" else SPACES[place](shape, dtype)

    sems = [pltpu.SemaphoreType.DMA((copies,))] if copies else []
    return pl.pallas_call(
        body,
        out_shape=[shape_of(*out) for out in outs],
        in_specs=[pl.BlockSpec(memory_space=SPACES[place]) for _, place in operands],
        out_specs=[pl.BlockSpec(memory_space=SPACES[place]) for _, _, place in outs],
        scratch_shapes=[pltpu.VMEM(s, d) for s, d in scratch] + sems,
        input_output_aliases=aliases or {},
        compiler_params=pltpu.CompilerParams(vmem_limit_bytes=VMEM_LIMIT),
        cost_estimate=pl.CostEstimate(
            flops=SIDE_COST if name in SIDE else TINY_COST if name in TINY else MAIN_COST,
            bytes_accessed=1000,
            transcendentals=0,
        ),
        name=name,
    )(
        *[
            pltpu.with_memory_space_constraint(array, pltpu.HBM) if place == "H" else array
            for array, place in operands
        ]
    )


def pairs_xor(axis, bit):
    return [(i, i ^ bit) for i in range(lax.axis_size(axis))]


class Order:
    def __init__(self):
        self.tokens = []

    def hold(self, *arrays):
        held = lax.optimization_barrier(tuple(arrays) + tuple(self.tokens))
        self.tokens = list(held)
        return held[: len(arrays)]

    def run(self, body, name, operands, *args, **kwargs):
        tokens, count = self.tokens, len(operands)

        def kernel(*refs):
            body(*refs[:count], *refs[count + len(tokens) :])

        operands = list(operands) + [(token, "A") for token in tokens]
        out = call(kernel, name, operands, *args, **kwargs)
        self.tokens = [out[-1]]
        return out


def add_kernel(held, sent, out):
    out[...] = held[...] + sent[...]


def add(order, held, sent):
    [out] = order.run(
        add_kernel, "add", [(held, "W"), (sent, "W")], [(held.shape, held.dtype, "W")]
    )
    return out


class Pipeline:
    def __init__(self, order, scal, count):
        self.order, self.scal, self.count = order, scal, count
        self.own, self.peer = [], []
        self.passed, self.outer, self.near, self.middle = {}, {}, {}, {}

    def put(self, own, peer):
        self.own.append(own)
        self.peer.append(lax.ppermute(peer, "dp", pairs_xor("dp", 1)))

    def run(self, kernel, name, arrays, scal=()):
        operands = [*scal, *[(array, "W") for array in arrays]]
        return self.order.run(kernel, name, operands, [(arrays[0].shape, BF16, "W")])[0]

    def pass_on(self, t):
        mine = [self.own[t], self.peer[t]] if t < self.count else []
        totals = [self.near[t - 2], self.middle[t - 2]] if t >= 2 else []
        arrays = mine + totals
        kernel = functools.partial(pass_kernel, bool(mine), bool(totals))
        self.passed[t] = self.run(kernel, "add", arrays, [self.scal])
        pairs = ([(0, 1), (3, 2)] if mine else []) + ([(1, 0), (2, 3)] if totals else [])
        self.outer[t] = lax.ppermute(self.passed[t], "section", pairs)

    def across(self, t):
        arrays = [self.own[t], self.peer[t], self.outer[t]]
        self.near[t] = self.run(near_kernel, "add", arrays)
        self.middle[t] = lax.ppermute(self.near[t], "section", [(1, 2), (2, 1)])

    def total(self, t):
        return self.passed[t + 2], self.outer[t + 2]


def shards(
    inputs,
    segments,
    cotangent,
    norm_gain,
    norm_shift,
    out_bias,
    attn_qkv,
    attn_out,
    attn_bias,
    mlp_in,
    mlp_out,
    mlp_bias,
):
    section = lax.axis_index("section")
    dp = lax.axis_index("dp")
    tensor = lax.axis_index("tensor")
    dp_count = lax.axis_size("dp")
    layers = attn_qkv.shape[0]
    rows, model = inputs.shape[2], inputs.shape[3]
    half = rows // 2
    shard = attn_qkv.shape[1]
    width = attn_out.shape[2]
    units = mlp_in.shape[2]
    heads = width // HEAD
    core = tensor % 2
    scal = (jnp.stack([core, dp, section % 2, section]).astype(jnp.int32), "S")
    paired = dp_count == 2
    order = Order()

    def places(place, arrays):
        return [(array, place) for array in arrays]

    table = jnp.concatenate([norm_gain, norm_shift, out_bias], axis=0)
    table = jnp.pad(table, ((0, 5), (0, 0)))[None]
    for bit in (1, 2):
        table = jnp.concatenate([table, lax.ppermute(table, "section", pairs_xor("section", bit))])
    table = (table, "V")

    qkv_t = attn_qkv.transpose(0, 2, 3, 1).reshape(layers, 3 * width, shard)
    out_t = attn_out.transpose(0, 2, 1)

    def sent(shared, direct):
        near = lax.ppermute(shared, "dp", pairs_xor("dp", 1))
        return [near, None, lax.ppermute(direct, "dp", pairs_xor("dp", 1))]

    def send_on(weights):
        if paired:
            [weights[-3]] = order.hold(weights[-3])
            weights[-2] = lax.ppermute(weights[-3], "section", pairs_xor("section", 1))

    def arrived(weights):
        if paired:
            [weights[-1]] = order.hold(weights[-1])

    def attn_gather(layer):
        if not paired:
            pack = jnp.concatenate([qkv_t[layer], out_t[layer]], axis=0).astype(BF16)
            return [lax.all_gather(pack, "dp", axis=1, tiled=True)]
        third = 4 * width // 3
        own, shared, direct = order.run(
            functools.partial(attn_pack, layer),
            "attn_pack",
            [scal, (qkv_t, "H"), (out_t, "H")],
            [((4 * width, shard), BF16, "H")] + [((third, shard), BF16, "V")] * 2,
            [((4 * width, shard), F32), ((4 * width, shard), BF16)],
            copies=7,
        )
        return [own, *sent(shared, direct)]

    def mlp_gather(layer):
        if not paired:
            return [
                lax.all_gather(mlp_in[layer].astype(BF16), "dp", axis=0, tiled=True),
                lax.all_gather(mlp_out[layer].astype(BF16), "dp", axis=1, tiled=True),
            ]
        third = 2 * shard // 3
        own_up, own_down, shared, direct = order.run(
            functools.partial(mlp_pack, layer),
            "mlp_pack",
            [scal, (mlp_in, "H"), (mlp_out, "H")],
            [((shard, units), BF16, "H"), ((units, shard), BF16, "H")]
            + [((third, units), BF16, "V")] * 2,
            [(shape, kind) for kind in (F32, BF16) for shape in ((shard, units), (units, shard))],
            copies=12,
        )
        return [own_up, own_down, *sent(shared, direct)]

    seg = lax.dynamic_index_in_dim(segments[:, 0], section, 0, keepdims=False)
    segs = [(seg[:, None], "V"), (seg[None, :], "V")]

    row_f32, row_low = ((rows, model), F32), ((rows, model), BF16)
    unit_f32, unit_low = ((rows, units), F32), ((rows, units), BF16)
    half_low = ((half, model), BF16)
    small_out = ((8, model), F32, "W")
    qkv_low, soft_f32 = ((3, rows, width), BF16), ((heads, rows, rows), F32)
    ctx_low, attn_full = ((rows, width), BF16), ((4 * width, model), BF16)
    up_full, down_full = ((model, units), BF16), ((units, model), BF16)

    def held(*shapes):
        return [shape + ("V",) for shape in shapes]

    def move_data(save=(), fetch=(), attn=None, mlp=None):
        pieces = attn or mlp or []

        def plan(scal, ins, outs):
            count = len(save) + len(fetch)
            pairs = list(zip(ins[:count], outs[:count]))
            if attn:
                pairs += attn_pieces(scal, ins[count:], outs[count])
            if mlp:
                ups, downs = mlp_pieces(scal, ins[count:], *outs[count:])
                pairs += ups + downs
            return pairs

        outs = [(array.shape, array.dtype, "H") for array in save]
        outs += [(array.shape, array.dtype, "V") for array in fetch]
        outs += held(attn_full) if attn else held(up_full, down_full) if mlp else []
        operands = places("V", save) + places("H", list(fetch) + list(pieces))
        return order.run(
            functools.partial(shuttle, plan, len(operands)),
            "shuttle",
            [scal, *operands],
            outs,
            copies=len(save) + len(fetch) + (11 if mlp else 4),
        )

    def nothing():
        return None

    def tensor_sum(mine, other, window=nothing, ahead=nothing, moves=((), (), ())):
        arrived = lax.ppermute(other, "tensor", pairs_xor("tensor", 1))
        ahead()
        move(*moves[0])
        near = add(order, mine, arrived)
        arrived = lax.ppermute(near, "tensor", pairs_xor("tensor", 2))
        window()
        move(*moves[1])
        total = add(order, near, arrived)
        arrived = lax.ppermute(total, "tensor", pairs_xor("tensor", 1))
        move(*moves[2])
        return [total, arrived]

    def fore_steps(mine, other):
        arrived = lax.ppermute(other, "tensor", pairs_xor("tensor", 1))
        yield
        near = add(order, mine, arrived)
        arrived = lax.ppermute(near, "tensor", pairs_xor("tensor", 2))
        yield
        total = add(order, near, arrived)
        arrived = lax.ppermute(total, "tensor", pairs_xor("tensor", 1))
        yield
        out, _ = order.run(
            functools.partial(output, 2 * layers),
            "output",
            [scal, table, *places("V", [x3, total, arrived])],
            [row_f32 + ("H",), ((8, 128), F32, "V")],
            [row_f32],
            copies=1,
        )
        yield out

    def attn_step(s, res, w):
        return order.run(
            functools.partial(attn_forward, s),
            "attn_forward",
            [scal, table, *places("V", res), *segs, *places("V", [attn_bias[s // 2], w])],
            held(*([row_f32] if s else []), row_low, qkv_low, soft_f32, ctx_low, half_low, half_low),
            [row_f32],
        )

    def mlp_step(s, res, up, down, cotangent=None):
        last = cotangent is not None
        operands = [*res, mlp_bias[s // 2][None], up, down] + ([cotangent] if last else [])
        if last:
            grads = mlp_shapes()
            outs = held(row_f32, half_low, half_low) + [small_out] + held(half_low, half_low)
            outs += grads
        else:
            grads = []
            outs = held(row_f32, row_low, unit_low, unit_f32, half_low, half_low)
        return order.run(
            functools.partial(mlp_forward, s, len(grads)),
            "mlp_forward",
            [scal, table, *places("V", operands)],
            outs,
            [row_f32] + ([(up_full[0], F32)] if last else []),
        )

    def mlp_shapes():
        if not paired:
            return [(down_full[0], BF16, "W"), (up_full[0], BF16, "W")]
        return [((units, shard), BF16, "W")] * 4

    def attn_shapes():
        if not paired:
            return [(attn_full[0], BF16, "W")]
        return [((4 * width, shard), BF16, "W")] * 2

    chunks = []
    pipeline = Pipeline(order, scal, 3 * layers)

    def add_chunks(parts, axis):
        if not paired:
            whole = lax.psum_scatter(parts[0], "dp", scatter_dimension=axis, tiled=True)
            chunks.append(lax.psum(whole, "section"))
            return
        for own, peer in zip(parts[0::2], parts[1::2]):
            pipeline.put(own, peer)

    emitted = {}

    def emit(kind, layer, index):
        shape = {"up": (shard, units), "down": (units, shard), "attn": (4 * width, shard)}[kind]
        token = ((8, 128), F32, "V")
        outs = [((layers,) + shape, F32, "H")]
        if kind == "attn":
            outs = [((layers, count, shard), F32, "H") for count in (3 * width, width)]
        before = emitted.get(kind, [])
        operands = list(pipeline.total(index))
        *emitted[kind], _ = order.run(
            functools.partial(emit_sums, kind, layer, len(before)),
            "emit",
            [scal, *places("W", operands), *places("H", before)],
            [*outs, token],
            [(shape, F32)],
            copies=3,
            aliases={1 + len(operands) + index: index for index in range(len(before))},
        )

    def small_sum(held):
        sent = lax.ppermute(held, "dp", pairs_xor("dp", 1))
        for bit in (1, 2):
            yield
            held = add(order, held, sent)
            sent = lax.ppermute(held, "section", pairs_xor("section", bit))
        yield
        yield order.run(
            functools.partial(unpack, layers),
            "unpack",
            [scal, (held, "W"), (sent, "W")],
            [((1, model), F32, "W")] * 3
            + [((layers, units), F32, "W"), ((2 * layers, width), F32, "W")],
            [((SMALL_ROWS, model), F32)],
        )

    def move(*indices):
        for index in indices:
            if index == FORE:
                fore.append(next(fore[0]))
            elif index == SMALL:
                small_steps.append(next(small_steps[0]))
            elif not paired:
                continue
            else:
                step, t = index
                if step == EMIT:
                    emit(("down", "up", "attn")[t % 3], layers - 1 - t // 3, t)
                else:
                    (pipeline.pass_on if step == PASS else pipeline.across)(t)

    def mlp_chunks(parts):
        add_chunks(parts[: len(parts) // 2], 1)
        add_chunks(parts[len(parts) // 2 :], 0)

    def back(body, name, s, operands, full, grads):
        return order.run(
            functools.partial(body, s),
            name,
            [scal, table, *places("V", operands)],
            held(row_f32) + [small_out] + held(half_low, half_low) + grads,
            [row_f32, (full[0], F32)],
        )

    box = {}

    def keep(names, values):
        box.update(zip(names, values))

    def kept(*names):
        return [box[name] for name in names]

    x0 = inputs.reshape(rows, model)
    pieces = {}

    def weigh(*steps):
        for step, s in steps:
            if step == PACK:
                pieces[s] = (mlp_gather if s % 2 else attn_gather)(s // 2)
            else:
                (send_on if step == ON else arrived)(pieces[s])

    weigh(*WEIGHTS[0])
    [w] = move_data(attn=pieces[0])
    low, qkv, soft, ctx, *halves = attn_step(0, [x0], w)

    def window():
        weigh(*WEIGHTS[2])
        keep(
            ("low0", "qkv0", "soft0", "ctx0", "up", "down"),
            move_data([low, qkv, soft, ctx], mlp=pieces[1]),
        )
        weigh(*WEIGHTS[3])

    total = tensor_sum(*halves, window, lambda: weigh(*WEIGHTS[1]))
    x1, low, active, slope, *halves = mlp_step(1, [x0, *total], box["up"], box["down"])

    def window():
        weigh(*WEIGHTS[5])
        keep(
            ("x1", "low1", "active1", "slope1", "w"),
            move_data([x1, low, active, slope], attn=pieces[2]),
        )
        weigh(*WEIGHTS[6])

    total = tensor_sum(*halves, window, lambda: weigh(*WEIGHTS[4]))
    x2, low, qkv, soft, ctx, *halves = attn_step(2, [x1, *total], box["w"])

    def window():
        weigh(*WEIGHTS[8])
        keep(
            ("x2", "low2", "qkv2", "soft2", "ctx2", "up", "down"),
            move_data([x2, low, qkv, soft, ctx], mlp=pieces[3]),
        )

    total = tensor_sum(*halves, window, lambda: weigh(*WEIGHTS[7]))
    g = cotangent.reshape(rows, model)
    x3, fore_mine, fore_other, small3, *rest = mlp_step(
        3, [x2, *total], box["up"], box["down"], g
    )
    fore = [fore_steps(fore_mine, fore_other)]

    def window():
        keep(
            ("low", "ctx", "qkv", "soft", "w"),
            move_data(fetch=kept("low2", "ctx2", "qkv2", "soft2"), attn=pieces[2]),
        )

    total = tensor_sum(*rest[:2], window, lambda: mlp_chunks(rest[2:]), MOVES[0])
    operands = [g, *total, x3, *kept("low", "qkv", "soft", "ctx", "w")]
    g, small2, *rest = back(
        attn_backward, "attn_backward", 2, operands, attn_full, attn_shapes()
    )

    def window():
        keep(
            ("x", "low", "active", "slope", "up", "down"),
            move_data(fetch=kept("x2", "low1", "active1", "slope1"), mlp=pieces[1]),
        )

    total = tensor_sum(*rest[:2], window, lambda: add_chunks(rest[2:], 1), MOVES[1])
    operands = [g, *total, *kept("x", "low", "active", "slope", "up", "down")]
    g, small1, *rest = back(mlp_backward, "mlp_backward", 1, operands, up_full, mlp_shapes())

    def window():
        keep(
            ("x", "low", "ctx", "qkv", "soft", "w"),
            move_data(fetch=kept("x1", "low0", "ctx0", "qkv0", "soft0"), attn=pieces[0]),
        )

    total = tensor_sum(*rest[:2], window, lambda: mlp_chunks(rest[2:]), MOVES[2])
    operands = [g, *total, *kept("x", "low", "qkv", "soft", "ctx", "w")]
    g, small0, *rest = back(
        attn_backward, "attn_backward", 0, operands, attn_full, attn_shapes()
    )
    total = tensor_sum(*rest[:2], ahead=lambda: add_chunks(rest[2:], 1), moves=MOVES[3])
    operands = [g, *total, x0]
    if paired:
        input_grad, small = order.run(
            input_backward_packed,
            "input_backward",
            [scal, table, *places("V", [*operands, small0, small1, small2, small3])],
            [row_f32 + ("H",), ((SMALL_ROWS, model), F32, "W")],
            [row_f32, ((8, model), F32)],
            copies=1,
        )
        small_steps = [small_sum(small)]
        move(*MOVES[4])
        [up_grad], [down_grad], (qkv_grad, out_grad) = (
            emitted[kind] for kind in ("up", "down", "attn")
        )
        gain_grad, shift_grad, bias_grad, mlp_rows, attn_rows = small_steps[4]
        attn_rows = attn_rows.reshape(layers, 2, width)
    else:
        input_grad, small = order.run(
            input_backward,
            "input_backward",
            [scal, table, *places("V", operands)],
            [row_f32 + ("H",), small_out],
            [row_f32],
            copies=1,
        )
        small = jnp.stack([small, small0, small1, small2, small3])
        small = lax.psum(small, ("section", "dp"))
        down_grad, up_grad, pack = [
            jnp.stack(chunks[3 + kind :: -3]).astype(F32) for kind in range(3)
        ]
        qkv_grad, out_grad = pack[:, : 3 * width], pack[:, 3 * width :]
        gain_grad, shift_grad, bias_grad = [
            lax.dynamic_slice_in_dim(rows_all, section, 1, 0)
            for rows_all in (small[:-1, 0], small[:-1, 1], small[1:, 2])
        ]
        mlp_rows = jnp.stack([small[2 * layer + 2, 3, :units] for layer in range(layers)])
        attn_rows = jnp.stack([small[2 * layer + 1, 3:5, :width] for layer in range(layers)])
    while len(fore) < 5:
        move(FORE)
    outputs = fore[4]
    qkv_grad = qkv_grad.reshape(layers, 3, width, shard).transpose(0, 3, 1, 2)

    return (
        outputs.reshape(inputs.shape),
        input_grad.reshape(inputs.shape),
        gain_grad,
        shift_grad,
        bias_grad,
        qkv_grad,
        out_grad.transpose(0, 2, 1),
        attn_rows,
        up_grad,
        down_grad,
        mlp_rows,
    )


def solution(mesh):
    placed = (
        P("section", "dp", None, None),
        P(None, "dp", None),
        P("section", "dp", None, None),
        P("section", None),
        P("section", None),
        P("section", None),
        P(None, "dp", None, "tensor"),
        P(None, "dp", "tensor"),
        P(None, None, "tensor"),
        P(None, "dp", "tensor"),
        P(None, "tensor", "dp"),
        P(None, "tensor"),
    )
    return jax.shard_map(
        shards,
        mesh=mesh,
        in_specs=placed,
        out_specs=(
            P("section", "dp", None, None),
            P("section", "dp", None, None),
            P("section", None),
            P("section", None),
            P("section", None),
            P(None, "dp", None, "tensor"),
            P(None, "dp", "tensor"),
            P(None, None, "tensor"),
            P(None, "dp", "tensor"),
            P(None, "tensor", "dp"),
            P(None, "tensor"),
        ),
        check_vma=False,
    )
```
